32 devices in a mesh: fsdp: 4 (over z), seq: 8 (over y, x, core).
Axes of the slice: x: 2, y: 2, z: 4, core: 2. Of those that a mesh axis runs over, the one named last changes fastest.
Arguments:
- tokens: bfloat16 [4096, 2048], P(('fsdp', 'seq')), may hold values from -6 to 6
- segments: int32 [4096], P(('fsdp', 'seq')), may hold values from 0 to 2, as said below
- routes: int32 [4096, 8], P(('fsdp', 'seq')), may hold values from 0 to 15, all different within a row; in each aligned block of 128 rows (0 to 127, 128 to 255, ...) at most 96 rows name the same one
- out_grad: bfloat16 [4096, 2048], P(('fsdp', 'seq')), may hold values from -6 to 6
- w_query: float32 [2048, 2048], P(('fsdp', 'seq')), may hold values from -0.125 to 0.125
- w_key: float32 [2048, 2048], P(('fsdp', 'seq')), may hold values from -0.125 to 0.125
- w_value: float32 [2048, 2048], P(('fsdp', 'seq')), may hold values from -0.125 to 0.125
- w_out: float32 [2048, 2048], P(('fsdp', 'seq')), may hold values from -3 to 3
- router: float32 [2048, 16], P(('fsdp', 'seq')), may hold values from -0.0625 to 0.0625
- attn_gain: float32 [2048], P(('fsdp', 'seq')), may hold values from 0.25 to 1.75
- q_gain: float32 [2048], P(('fsdp', 'seq')), may hold values from 0.25 to 1.75
- k_gain: float32 [2048], P(('fsdp', 'seq')), may hold values from 0.25 to 1.75
- ffn_gain: float32 [2048], P(('fsdp', 'seq')), may hold values from 0.25 to 1.75
- expert_gate_up: float32 [32, 2048, 2, 512], P(('fsdp', 'seq')), may hold values from -0.125 to 0.125
- expert_down: float32 [32, 512, 2048], P(('fsdp', 'seq')), may hold values from -6 to 6
Outputs:
- output: bfloat16 [4096, 2048], P(('fsdp', 'seq'))
- input_grad: bfloat16 [4096, 2048], P(('fsdp', 'seq'))
- w_query_grad: float32 [2048, 2048], P(('fsdp', 'seq'))
- w_key_grad: float32 [2048, 2048], P(('fsdp', 'seq'))
- w_value_grad: float32 [2048, 2048], P(('fsdp', 'seq'))
- w_out_grad: float32 [2048, 2048], P(('fsdp', 'seq'))
- router_grad: float32 [2048, 16], P(('fsdp', 'seq'))
- attn_gain_grad: float32 [2048], P(('fsdp', 'seq'))
- q_gain_grad: float32 [2048], P(('fsdp', 'seq'))
- k_gain_grad: float32 [2048], P(('fsdp', 'seq'))
- ffn_gain_grad: float32 [2048], P(('fsdp', 'seq'))
- expert_gate_up_grad: float32 [32, 2048, 2, 512], P(('fsdp', 'seq'))
- expert_down_grad: float32 [32, 512, 2048], P(('fsdp', 'seq'))
The draws below stay inside these ranges and needn't reach their ends.
Inputs may be any that keep to these rules, and one draw needn't show every extreme that they name: `segments`: segment numbers restart in each sequence of 1024 tokens: three documents 0, 1, 2 in order, the first and the last each 1 to 64 tokens long. `routes`: each row names 8 different experts. Within the 128 rows of one device no expert is named by more than 96 rows, and in some device one is named by exactly 96.
All inputs are finite; a program needn't handle non-finite values.
Results may differ from the reference program's by a relative error of at most 0.02.
The reference program's roundings to bfloat16 on the way count: a program that leaves them out, or rounds other values in their place, can miss the bound.
Values may be sent and summed in bfloat16 or wider, within the bound.
No kernel may reach another device: no remote copies, remote signals or barrier semaphores. Data moves between devices by JAX's collectives and lax.ppermute only.
A program may use at most 448 MiB of HBM per device.

```python
import math
import jax
import jax.numpy as jnp
import numpy as np
from jax import lax

HEADS = 16
HEAD_DIM = 128
D = 2048
TOPK = 8
SPLIT = 2
FH = 512
TOK_DEV = 128
SEQS = 4
SEQ_LEN = 1024
TOKENS = 4096
EXPERTS = 16
SHARDS = 32
CAP = 96
N_SEQ = 8


def draw_segments(key, part):
    key = jax.random.fold_in(key, 7)
    first_key, last_key = jax.random.split(key)
    head_length = jax.random.randint(first_key, (SEQS, 1), 1, TOK_DEV // 2 + 1)
    tail_length = jax.random.randint(last_key, (SEQS, 1), 1, TOK_DEV // 2 + 1)
    places = jnp.arange(SEQ_LEN, dtype=jnp.int32)[None, :]
    numbers = (places >= head_length).astype(jnp.int32) + (places >= SEQ_LEN - tail_length).astype(jnp.int32)
    return numbers.reshape(TOKENS)


def with_spikes(values, stream_key, source, target, blocks, factor):
    owner, partner = [(jnp.arange(values.shape[axis_at]) // (values.shape[axis_at] // blocks)).reshape([-1 if axis == axis_at else 1 for axis in range(values.ndim)]) for axis_at in (source, target)]
    chosen = jax.random.permutation(stream_key, blocks)[partner]
    strong = (owner == chosen) | (owner == (partner + blocks // 2) % blocks)
    return jnp.where(strong, factor * values, values)


def levels(rng, extent, pieces, low, largest):
    factor_of = 1.0
    for axis_at, parts in pieces:
        heights = jax.random.uniform(jax.random.fold_in(jax.random.fold_in(rng, 6), axis_at), (parts,), jnp.float32, low / len(pieces), largest / len(pieces))
        factor_of = factor_of * jnp.repeat(jnp.exp(heights), extent[axis_at] // parts).reshape((-1,) + (1,) * (len(extent) - 1 - axis_at))
    return factor_of


def shared_out(stream_key, own, number, rows, amount, top, bound, slope):
    sequence = jax.random.permutation(stream_key, amount)
    heavy_load, common = portions_of(amount, rows * top, bound, slope, True), portions_of(amount, rows * top, bound, slope, False)
    places = jnp.arange(amount)

    def named(tallies, offset_by):
        used = int((tallies > 0).sum())
        fixed = max(1, used // 4)
        moved = fixed + (places - fixed + offset_by * (used - fixed)) % max(1, amount - fixed)
        return jnp.zeros((amount,), jnp.int32).at[sequence[jnp.where(places < fixed, places, moved)]].set(jnp.asarray(tallies, jnp.int32))

    tallies = jnp.where(number % 4 == 0, named(heavy_load, number // 4), named(common, number - number // 4 - 1))
    mixed = jax.random.permutation(jax.random.fold_in(own, 3), amount)
    giver, receiver = mixed[0:amount // 2 * 2:2], mixed[1:amount // 2 * 2:2]
    margin = jnp.minimum(tallies[giver] - 1, bound - tallies[receiver]) // 2
    margin = jnp.where((giver == sequence[0]) | (receiver == sequence[0]) | (tallies[receiver] == 0), 0, jnp.maximum(margin, 0))
    moved = jax.random.randint(jax.random.fold_in(own, 4), (amount // 2,), 0, 1 << 20) % (margin + 1)
    tallies = tallies.at[giver].add(-moved).at[receiver].add(moved)
    labels = jnp.searchsorted(jnp.cumsum(tallies), jnp.arange(rows * top), side="right").astype(jnp.int32)
    grid = labels.reshape(top, rows).T
    grid = grid[jax.random.permutation(jax.random.fold_in(own, 1), rows)]
    offset_by = jax.random.randint(jax.random.fold_in(own, 2), (rows, 1), 0, top)
    return jnp.take_along_axis(grid, (jnp.arange(top)[None, :] + offset_by) % top, axis=1)


def portions_of(count, total, limit, slope, full):
    weights = [(1 << 20) // math.isqrt(grade ** slope) + 1 for grade in range(1, count + 1)]
    largest = limit if full else min(limit, max(-(-total // count), total * weights[0] // sum(weights)))
    least = 1 if total - largest >= count - 1 else 0
    given, surplus = [largest] + [least] * (count - 1), total - largest - least * (count - 1)
    while surplus > 0:
        movable = [i for i in range(1, count) if given[i] < largest] or [i for i in range(1, count) if given[i] < limit]
        pool, left = sum([weights[i] for i in movable]), surplus
        for i in movable:
            extra = min(limit - given[i], max(1, left * weights[i] // pool), surplus)
            given[i] = given[i] + extra
            surplus = surplus - extra
    return np.array(given)


def centred(key, dims, spread, limit, shards=(), kind=jnp.bfloat16):
    level = levels(key, dims, shards, -0.22, 0.18) if shards else 1.0
    values = jax.random.normal(key, dims, jnp.float32) * spread * level
    return jnp.minimum(jnp.maximum(values, -limit), limit).astype(kind)


def heavy_noise(rng, dims, deviation, limit, cuts, heavy, kind=jnp.bfloat16):
    values = deviation * jax.random.normal(rng, dims, jnp.float32)
    if cuts:
        values = values * levels(rng, dims, cuts, -0.22, 0.18)
    return jnp.clip(with_spikes(values, jax.random.fold_in(rng, 3), *heavy), -limit, limit).astype(kind)


def setup_inputs(seed: int = 0) -> dict:
    key_of = jax.random.split(jax.random.key(seed), 16)
    tokens = heavy_noise(key_of[0], (TOKENS, D), 1.0, 6.0, ((0, 32),), (0, 1, 32, 2.75))
    segments = draw_segments(jax.random.fold_in(key_of[15], 71), 0)
    routes_keys = jax.random.split(jax.random.fold_in(key_of[2], 1), TOKENS // TOK_DEV)
    routes_turns = jax.random.permutation(jax.random.fold_in(key_of[2], 3), TOKENS // TOK_DEV)
    routes = jax.vmap(lambda own, number: shared_out(jax.random.fold_in(key_of[2], 2), own, number, TOK_DEV, EXPERTS, TOPK, CAP, 1))(routes_keys, routes_turns).reshape((TOKENS, TOPK))
    out_grad = centred(key_of[3], (TOKENS, D), 1.0, 6.0, ((0, 32),))
    w_query = centred(key_of[4], (D, D), D ** -0.5, 0.125, ((0, 32),), jnp.float32)
    w_key = centred(key_of[5], (D, D), D ** -0.5, 0.125, ((0, 32),), jnp.float32)
    w_value = centred(key_of[6], (D, D), D ** -0.5, 0.125, ((0, 32),), jnp.float32)
    w_out = centred(key_of[7], (D, D), (max(1, D // 512)) ** -0.5, 3.0, ((0, 32),), jnp.float32)
    router = centred(key_of[8], (D, EXPERTS), (4 * D) ** -0.5, 0.0625, ((0, 32),), jnp.float32)
    attn_gain = jnp.clip(1.0 + 0.15 * jax.random.normal(key_of[9], (D,), jnp.float32), 0.25, 1.75)
    q_gain = jnp.clip(1.0 + 0.15 * jax.random.normal(key_of[10], (D,), jnp.float32), 0.25, 1.75)
    k_gain = jnp.clip(1.0 + 0.15 * jax.random.normal(key_of[11], (D,), jnp.float32), 0.25, 1.75)
    ffn_gain = jnp.clip(1.0 + 0.15 * jax.random.normal(key_of[12], (D,), jnp.float32), 0.25, 1.75)
    expert_gate_up = centred(key_of[13], (SHARDS, D, 2, FH), D ** -0.5, 0.125, ((0, 32),), jnp.float32)
    expert_down = centred(key_of[14], (SHARDS, FH, D), 1 ** -0.5, 6.0, ((0, 32),), jnp.float32)
    return {"tokens": tokens, "segments": segments, "routes": routes, "out_grad": out_grad, "w_query": w_query, "w_key": w_key, "w_value": w_value, "w_out": w_out, "router": router, "attn_gain": attn_gain, "q_gain": q_gain, "k_gain": k_gain, "ffn_gain": ffn_gain, "expert_gate_up": expert_gate_up, "expert_down": expert_down}


EPSILON = 1e-05
THETA = 10000.0
HIGHEST = lax.Precision.HIGHEST

@jax.custom_vjp
def low(v):
    return lax.optimization_barrier(v.astype(jnp.bfloat16)).astype(jnp.float32)

@jax.custom_vjp
def low_back(v):
    return v

def low_keep(v):
    return (low(v), None)

def low_pass(kept, grad):
    return (grad,)

def back_keep(v):
    return (v, None)

def back_low(kept, grad):
    return (low(grad),)
low.defvjp(low_keep, low_pass)
low_back.defvjp(back_keep, back_low)

def rms_scale(values, gain):
    inverse = lax.rsqrt(lax.optimization_barrier(jnp.mean(values * values, axis=-1, keepdims=True)) + EPSILON)
    return values * inverse * gain

def rotate(values, positions):
    row_count = values.shape[0]
    half_width = HEAD_DIM // 2
    frequency = THETA ** (-jnp.arange(half_width, dtype=jnp.float32) * 2.0 / HEAD_DIM)
    angles = positions.astype(jnp.float32)[:, None] * frequency[None, :]
    cosine_table = jnp.cos(angles)[:, None, :]
    sine_table = jnp.sin(angles)[:, None, :]
    shaped = values.reshape(row_count, HEADS, HEAD_DIM)
    first_half = shaped[..., :half_width]
    second_half = shaped[..., half_width:]
    turned = jnp.concatenate([first_half * cosine_table - second_half * sine_table, second_half * cosine_table + first_half * sine_table], axis=-1)
    return turned.reshape(row_count, HEADS * HEAD_DIM)

def sequence_layer(values, seg_block, route_block, weights):
    wq, wk, wv, wo, wr, ga, gq, gk, gf, wgu, wdn = weights
    places = jnp.arange(SEQ_LEN, dtype=jnp.int32)
    normed = low(rms_scale(values, ga))
    query_proj = low_back(jnp.dot(normed, wq, precision=HIGHEST))
    key_proj = low_back(jnp.dot(normed, wk, precision=HIGHEST))
    value_proj = low(low_back(jnp.dot(normed, wv, precision=HIGHEST)))
    queries = low(rotate(rms_scale(query_proj, gq), places))
    keys_all = low(rotate(rms_scale(key_proj, gk), places))
    query_heads = queries.reshape(SEQ_LEN, HEADS, HEAD_DIM)
    key_heads = keys_all.reshape(SEQ_LEN, HEADS, HEAD_DIM)
    value_heads = value_proj.reshape(SEQ_LEN, HEADS, HEAD_DIM)
    scores = low_back(jnp.einsum('thd,uhd->htu', query_heads, key_heads, precision=HIGHEST) * HEAD_DIM ** (-0.5))
    allowed = (places[None, :] <= places[:, None]) & (seg_block[None, :] == seg_block[:, None])
    masked = jnp.where(allowed[None], scores, -1e+30)
    attn_probs = low(jax.nn.softmax(masked, axis=-1))
    attended = jnp.einsum('htu,uhd->thd', attn_probs, value_heads, precision=HIGHEST).reshape(SEQ_LEN, D)
    attended = low(low_back(attended))
    proj_out = low_back(jnp.dot(attended, wo, precision=HIGHEST))
    middle = values + proj_out
    mixed = low(rms_scale(middle, gf))
    logits = low_back(jnp.dot(mixed, wr, precision=HIGHEST))
    expert_probs = jax.nn.softmax(logits, axis=-1)
    gates = jnp.take_along_axis(expert_probs, route_block, axis=1)
    expert_ids = route_block.reshape(-1)
    onehot = (expert_ids[:, None] == jnp.arange(EXPERTS, dtype=jnp.int32)[None, :]).astype(jnp.int32)
    slot_ids = lax.optimization_barrier(jnp.sum((jnp.cumsum(onehot, axis=0) - 1) * onehot, axis=1)).astype(jnp.int32)
    owners = (jnp.arange(SEQ_LEN * TOPK, dtype=jnp.int32) // TOPK).astype(jnp.int32)
    index_table = jnp.full((EXPERTS, N_SEQ * CAP), SEQ_LEN, jnp.int32).at[expert_ids, slot_ids].set(owners)
    padded = jnp.concatenate([mixed, jnp.zeros((1, D), jnp.float32)], axis=0)
    rows_in = padded[index_table]
    summed = jnp.zeros((EXPERTS, N_SEQ * CAP, D), jnp.float32)
    for part in range(SPLIT):
        gate_up = low_back(jnp.einsum('ecd,edkf->eckf', rows_in, wgu[:, part], precision=HIGHEST))
        hidden = low(jax.nn.silu(gate_up[:, :, 0]) * gate_up[:, :, 1])
        result = low(low_back(jnp.einsum('ecf,efd->ecd', hidden, wdn[:, part], precision=HIGHEST)))
        summed = summed + result
    picked = summed[expert_ids, slot_ids].reshape(SEQ_LEN, TOPK, D)
    mixture = lax.optimization_barrier(jnp.sum(gates[:, :, None] * picked, axis=1))
    return middle + mixture

def reference(tokens, segments, routes, out_grad, w_query, w_key, w_value, w_out, router, attn_gain, q_gain, k_gain, ffn_gain, expert_gate_up, expert_down):
    inputs = tokens.astype(jnp.float32)
    seg_blocks = segments.reshape(SEQS, SEQ_LEN)
    route_blocks = routes.reshape(SEQS, SEQ_LEN, TOPK)

    def forward(values, wq, wk, wv, wo, wr, ga, gq, gk, gf, wgu, wdn):
        weights = (low(wq), low(wk), low(wv), low(wo), low(wr), low(ga), low(gq), low(gk), low(gf), low(wgu).reshape(EXPERTS, SPLIT, D, 2, FH), low(wdn).reshape(EXPERTS, SPLIT, FH, D))

        def one_sequence(block):
            return sequence_layer(block[0], block[1], block[2], weights)
        outcome = lax.map(jax.checkpoint(one_sequence), (values.reshape(SEQS, SEQ_LEN, D), seg_blocks, route_blocks))
        return outcome.reshape(TOKENS, D)
    result, pullback = jax.vjp(forward, inputs, w_query, w_key, w_value, w_out, router, attn_gain, q_gain, k_gain, ffn_gain, expert_gate_up, expert_down)
    grads = pullback(out_grad.astype(jnp.float32))
    return (result.astype(jnp.bfloat16), grads[0].astype(jnp.bfloat16), grads[1], grads[2], grads[3], grads[4], grads[5], grads[6], grads[7], grads[8], grads[9], grads[10], grads[11])
```

```python
import jax
import jax.numpy as jnp
from jax import lax
from jax.experimental import pallas as pl
from jax.experimental.pallas import tpu as pltpu
from jax.sharding import PartitionSpec as P

HEADS = 16
SPLIT = 2
EPSILON = 1e-05
THETA = 10000.0
BOTH = ("fsdp", "seq")
BF16 = jnp.bfloat16
F32 = jnp.float32


def rows_by_rows(left, right):
    return lax.dot_general(left, right, (((0,), (0,)), ((), ())), preferred_element_type=F32)


def times_transposed(left, right):
    return lax.dot_general(left, right, (((1,), (1,)), ((), ())), preferred_element_type=F32)


def times(left, right):
    return jnp.dot(left, right, preferred_element_type=F32)


def inverse_rms(values):
    return lax.rsqrt(jnp.mean(values * values, axis=-1, keepdims=True) + EPSILON)


def rope_tables(positions, head_width):
    half_width = head_width // 2
    frequency = THETA ** (-jnp.arange(half_width, dtype=F32) * 2.0 / head_width)
    angles = positions.astype(F32)[:, None] * frequency[None, :]
    return jnp.cos(angles)[:, None, :], jnp.sin(angles)[:, None, :]


def rope(values, tables, heads):
    rows, width = values.shape
    cosine, sine = tables
    shaped = values.reshape(rows, heads, width // heads)
    half = width // heads // 2
    a, b = shaped[..., :half], shaped[..., half:]
    turned = jnp.concatenate([a * cosine - b * sine, b * cosine + a * sine], axis=-1)
    return turned.reshape(rows, width)


def rope_back(values, tables, heads):
    cosine, sine = tables
    return rope(values, (cosine, -sine), heads)


def exchange(x, mask, size):
    return lax.ppermute(x, "seq", [(i, i ^ mask) for i in range(size)])


def link_bits(size):
    bits, b = [], 2
    while b < size:
        bits.append(b)
        b *= 2
    return bits


def mask_order(size):
    masks = [0]
    for b in link_bits(size):
        masks = masks + [m | b for m in masks]
    return masks


def set_bits(mask):
    return [1 << i for i in range(mask.bit_length()) if mask >> i & 1]


def by_count(size):
    return sorted(mask_order(size), key=lambda m: (len(set_bits(m)), m))


def half_of(pieces, i):
    if len(pieces) == 2:
        return pieces[i]
    rows = pieces[0].shape[0] // 2
    return pieces[0][i * rows : (i + 1) * rows]


def gather_first(x, size):
    return {m: [x if m == 0 else exchange(x, m, size)] for m in [0] + link_bits(size)}


def gather_rest(pieces, size):
    pieces = dict(pieces)
    for m in by_count(size):
        bits = set_bits(m)
        if len(bits) > 1:
            low, high = bits[0], bits[-1]
            pieces[m] = [
                exchange(half_of(pieces[m ^ high], 0), high, size),
                exchange(half_of(pieces[m ^ low], 1), low, size),
            ]
    return pieces


def gather_one_way(pieces, size, high):
    pieces = dict(pieces)
    for m in by_count(size):
        bits = set_bits(m)
        if len(bits) > 1:
            b = bits[-1] if high else bits[0]
            pieces[m] = [exchange(pieces[m ^ b][0], b, size)]
    return pieces


def gather_pieces(x, size):
    return gather_rest(gather_first(x, size), size)


def flat(pieces):
    return [a for p in pieces.values() for a in p]


def other_core(pieces, size):
    return {m: [exchange(a, 1, size) for a in p] for m, p in pieces.items()}


def add_blocks(outputs, dtypes, unit):
    arrays, specs, index = [], [], {}
    for out in outputs:
        for terms in out:
            for array, block in terms:
                width = array.shape[1]
                index[(id(array), block)] = len(arrays)
                arrays.append(array)
                specs.append(pl.BlockSpec((unit, width), lambda i, block=block: (block, 0)))

    where = [[[index[(id(a), k)] for a, k in terms] for terms in out] for out in outputs]
    count = len(arrays)

    def kernel(*refs):
        for out_ref, blocks in zip(refs[count:], where):
            for i, terms in enumerate(blocks):
                total = refs[terms[0]][...].astype(F32)
                for t in terms[1:]:
                    total = total + refs[t][...].astype(F32)
                out_ref[i * unit : (i + 1) * unit, :] = total.astype(out_ref.dtype)

    shapes = [
        jax.ShapeDtypeStruct((len(out) * unit, width), dtype) for out, dtype in zip(outputs, dtypes)
    ]
    bytes_moved = sum(unit * width * 2 for _ in arrays) * 2
    return pl.pallas_call(
        kernel,
        grid=(1,),
        out_shape=shapes,
        in_specs=specs,
        out_specs=[pl.BlockSpec(s.shape, lambda i: (0, 0)) for s in shapes],
        compiler_params=pltpu.CompilerParams(vmem_limit_bytes=48 << 20),
        cost_estimate=pl.CostEstimate(flops=0, bytes_accessed=bytes_moved, transcendentals=0),
    )(*arrays)


def wait_first(outs, arrays):
    if arrays is None:
        return outs
    array, block = outs[0][0][-1]
    outs[0][0][-1] = (after(array, *arrays()), block)
    return outs


def scatter_sum(groups, size, unit, dtypes, hold=None, ties=None):
    ties = ties or {}
    order = by_count(size)
    at = {m: i for i, m in enumerate(mask_order(size))}
    extra = {(m, k): [] for m in order for k in range(len(groups))}

    def terms(m, k):
        keep, got, stride, offset, _ = groups[k]
        block = at[m] * stride + offset
        return [(keep, block), (got, block)] + extra[(m, k)]

    level = max(len(set_bits(m)) for m in order)
    while level > 0:
        routes = {}
        for m in order:
            bits = set_bits(m)
            if len(bits) == level:
                for k, g in enumerate(groups):
                    routes.setdefault((m, bits[-1] if g[4] else bits[0]), []).append(k)
        outs = [[terms(m, k) for k in members] for (m, _), members in routes.items()]
        outs = wait_first(outs, ties.get(level))
        sums = add_blocks(outs, [BF16] * len(outs), unit)
        if hold is not None:
            sums = hold(level, sums)
        for ((m, b), members), x in zip(routes.items(), sums):
            arrived = exchange(x, b, size)
            for i, k in enumerate(members):
                extra[(m ^ b, k)].append((arrived, i))
        level -= 1
    outs = wait_first([[terms(0, k)] for k in range(len(groups))], ties.get(0))
    sums = add_blocks(outs, dtypes, unit)
    return sums if hold is None else hold(0, sums)


def expert_rows(m_parts, c_all, c_rows, gates, row, gu, down):
    width = gu.shape[0]
    hidden = down.shape[0]
    rows = sum(n for _, _, n in m_parts)

    def inputs(parts):
        arrays = []
        for a, _, _ in parts:
            if not any(a is b for b in arrays):
                arrays.append(a)
        places, at = [], 0
        for a, first, n in parts:
            places.append(([i for i, b in enumerate(arrays) if b is a][0], first, n, at))
            at += n
        return arrays, places

    m_arrays, m_places = inputs(m_parts)
    nc = c_rows.shape[0]
    nm, each = len(m_arrays), rows // nc
    step = 256
    steps = rows // step
    small = 16

    def kernel(*refs):
        m_in = refs[:nm]
        c_in, table, gate_in, gu_in, dn_in = refs[nm : nm + 5]
        mix_out, dmx_out, dots_ref, m_out, c_out, hid_out, dgu_out = refs[nm + 5 : nm + 12]
        (m_s, c_s, gu_w, dn_w, hid_s, mix_s, dmx_s, dgu_s, g_s, q_s, gate_ref,
         m_sem, c_sem, w_sem, o_sem) = refs[nm + 12 :]

        copies_m = [
            pltpu.make_async_copy(
                m_in[k].at[pl.ds(first, n)], m_s.at[pl.ds(at, n)], m_sem.at[i]
            )
            for i, (k, first, n, at) in enumerate(m_places)
        ]
        copies_c = [
            pltpu.make_async_copy(
                c_in.at[pl.ds(pl.multiple_of(table[i], each), each)],
                c_s.at[pl.ds(i * each, each)],
                c_sem.at[i],
            )
            for i in range(nc)
        ]
        c_places = [(0, 0, each, i * each) for i in range(nc)]
        g_copy = pltpu.make_async_copy(gate_in.at[pl.ds(row, rows)], gate_ref, w_sem.at[2])
        w_gu = pltpu.make_async_copy(gu_in, gu_w, w_sem.at[0])
        w_dn = pltpu.make_async_copy(dn_in, dn_w, w_sem.at[1])
        def of_block(copies, places, b):
            return [c for c, p in zip(copies, places) if b * step <= p[3] < (b + 1) * step]

        for c in of_block(copies_m, m_places, 0):
            c.start()
        w_gu.start()
        g_copy.start()

        def sends(b):
            here = pl.ds(b * step, step)
            return [
                pltpu.make_async_copy(dmx_s.at[here], dmx_out.at[here], o_sem.at[2 * b]),
                pltpu.make_async_copy(mix_s.at[here], mix_out.at[here], o_sem.at[2 * b + 1]),
            ]

        n = 2 * steps
        whole = [
            pltpu.make_async_copy(m_s, m_out, o_sem.at[n]),
            pltpu.make_async_copy(c_s, c_out, o_sem.at[n + 1]),
            pltpu.make_async_copy(hid_s, hid_out, o_sem.at[n + 2]),
            pltpu.make_async_copy(dgu_s, dgu_out, o_sem.at[n + 3]),
        ]

        def block(b, carry):
            r = pl.ds(pl.multiple_of(b * step, step), step)
            for k in range(steps):

                @pl.when(b == k)
                def _():
                    for c in of_block(copies_m, m_places, k):
                        c.wait()
                    if k == 0:
                        w_gu.wait()
                        g_copy.wait()
                        w_dn.start()
                        for c in of_block(copies_c, c_places, 0):
                            c.start()
                    if k + 1 < steps:
                        for c in of_block(copies_m, m_places, k + 1):
                            c.start()

            g_s[...] = times(m_s[r, :], gu_w[...])
            for k in range(steps):

                @pl.when(b == k)
                def _():
                    for c in of_block(copies_c, c_places, k):
                        c.wait()
                    if k == 0:
                        w_dn.wait()
                    if k + 1 < steps:
                        for c in of_block(copies_c, c_places, k + 1):
                            c.start()
                    else:
                        whole[0].start()
                        whole[1].start()

            q_s[...] = times_transposed(c_s[r, :], dn_w[...])
            for s in range(step // small):
                here = slice(s * small, (s + 1) * small)
                out = pl.ds(pl.multiple_of(b * step + s * small, small), small)
                scale = gate_ref[out, :]
                g = g_s[here, :hidden]
                u = g_s[here, hidden:]
                q = q_s[here, :]
                sig = jax.nn.sigmoid(g)
                act = g * sig
                hid = act * u
                dots_ref[out, :] = jnp.sum(hid * q, axis=1, keepdims=True)
                hid_s[out, :] = (hid * scale).astype(BF16)
                dh = q * scale
                dgu_s[out, :hidden] = (dh * u * (sig + act * (1.0 - sig))).astype(BF16)
                dgu_s[out, hidden:] = (dh * act).astype(BF16)
            dmx_s[r, :] = times_transposed(dgu_s[r, :], gu_w[...]).astype(BF16)
            mix_s[r, :] = times(hid_s[r, :], dn_w[...]).astype(BF16)
            for k in range(steps):

                @pl.when(b == k)
                def _():
                    for c in sends(k):
                        c.start()

            return carry

        lax.fori_loop(0, steps, block, 0)
        whole[2].start()
        whole[3].start()
        for c in whole + [c for k in range(steps) for c in sends(k)]:
            c.wait()

    anywhere = pl.BlockSpec(memory_space=pl.ANY)
    vmem = pl.BlockSpec(memory_space=pltpu.VMEM)
    sds = jax.ShapeDtypeStruct
    return pl.pallas_call(
        kernel,
        out_shape=[
            sds((rows, width), BF16),
            sds((rows, width), BF16),
            sds((rows, 1), F32),
            sds((rows, width), BF16),
            sds((rows, width), BF16),
            sds((rows, hidden), BF16),
            sds((rows, 2 * hidden), BF16),
        ],
        in_specs=[anywhere] * (nm + 1)
        + [pl.BlockSpec(memory_space=pltpu.SMEM)]
        + [anywhere] * 3,
        out_specs=[anywhere] * 2 + [vmem] + [anywhere] * 4,
        scratch_shapes=[
            pltpu.VMEM((rows, width), BF16),
            pltpu.VMEM((rows, width), BF16),
            pltpu.VMEM((width, 2 * hidden), BF16),
            pltpu.VMEM((hidden, width), BF16),
            pltpu.VMEM((rows, hidden), BF16),
            pltpu.VMEM((rows, width), BF16),
            pltpu.VMEM((rows, width), BF16),
            pltpu.VMEM((rows, 2 * hidden), BF16),
            pltpu.VMEM((step, 2 * hidden), F32),
            pltpu.VMEM((step, hidden), F32),
            pltpu.VMEM((rows, 1), F32),
            pltpu.SemaphoreType.DMA((len(m_places),)),
            pltpu.SemaphoreType.DMA((nc,)),
            pltpu.SemaphoreType.DMA((3,)),
            pltpu.SemaphoreType.DMA((2 * steps + 4,)),
        ],
        compiler_params=pltpu.CompilerParams(vmem_limit_bytes=60 << 20),
        cost_estimate=pl.CostEstimate(
            flops=2 * rows * width * hidden * 6, bytes_accessed=24 << 20, transcendentals=0
        ),
    )(*m_arrays, c_all, c_rows, gates, gu, down)


def gate_up_weights(lefts, rights, before=None, rest=None):
    rows, width = lefts[0].shape
    cols = rights[0].shape[1]
    n, tile = len(lefts), 512
    steps = width // tile // 2
    skip = 0 if rest is None else steps

    def kernel(*refs):
        total = rows_by_rows(refs[0][...], refs[n][...])
        for i in range(1, n):
            total = total + rows_by_rows(refs[i][...], refs[n + i][...])
        out = refs[-1]
        for k in range(2):
            part = total[:, k * (cols // 2) : (k + 1) * (cols // 2)]
            out[:, k, :] = part if before is None else part + refs[2 * n][:, k, :]

    block = pl.BlockSpec((tile, 2, cols // 2), lambda i: (i + skip, 0, 0))
    extra = [] if before is None else [before]
    old = [] if rest is None else [rest]
    return pl.pallas_call(
        kernel,
        grid=(steps,),
        out_shape=jax.ShapeDtypeStruct((width, 2, cols // 2), F32),
        in_specs=[pl.BlockSpec((rows, tile), lambda i: (0, i + skip))] * n
        + [pl.BlockSpec((rows, cols), lambda i: (0, 0))] * n
        + [block] * len(extra)
        + [pl.BlockSpec(memory_space=pl.ANY)] * len(old),
        out_specs=block,
        input_output_aliases={2 * n + len(extra): 0} if old else {},
        compiler_params=pltpu.CompilerParams(vmem_limit_bytes=58 << 20),
        cost_estimate=pl.CostEstimate(
            flops=n * rows * width * cols, bytes_accessed=16 << 20, transcendentals=0
        ),
    )(*lefts, *rights, *extra, *old)


def down_weights(lefts, rights, before=None):
    rows, hidden = lefts[0].shape
    width = rights[0].shape[1]
    n, tile = len(lefts), 512

    def kernel(*refs):
        total = rows_by_rows(refs[0][...], refs[n][...])
        for i in range(1, n):
            total = total + rows_by_rows(refs[i][...], refs[n + i][...])
        refs[-1][...] = total if before is None else total + refs[2 * n][...]

    block = pl.BlockSpec((hidden, tile), lambda i: (0, i))
    extra = [] if before is None else [before]
    return pl.pallas_call(
        kernel,
        grid=(width // tile,),
        out_shape=jax.ShapeDtypeStruct((hidden, width), F32),
        in_specs=[pl.BlockSpec((rows, hidden), lambda i: (0, 0))] * n
        + [pl.BlockSpec((rows, tile), lambda i: (0, i))] * n
        + [block] * len(extra),
        out_specs=block,
        compiler_params=pltpu.CompilerParams(vmem_limit_bytes=58 << 20),
        cost_estimate=pl.CostEstimate(
            flops=2 * n * rows * width * hidden, bytes_accessed=24 << 20, transcendentals=0
        ),
    )(*lefts, *rights, *extra)


def after(x, *others):
    return lax.optimization_barrier((x, *others))[0]


def flip_slots(x, size, me):
    n = len(link_bits(size)) + 1
    for axis, b in enumerate([1] + link_bits(size)[::-1]):
        x = jnp.where((me & b) != 0, jnp.flip(x, axis), x)
    return x, n


def to_slots(x, size, me):
    n = len(link_bits(size)) + 1
    y = jnp.moveaxis(x.reshape((2,) * n + x.shape[1:]), n - 1, 0)
    return flip_slots(y, size, me)[0].reshape(x.shape)


def from_slots(x, size, me):
    n = len(link_bits(size)) + 1
    y = flip_slots(x.reshape((2,) * n + x.shape[1:]), size, me)[0]
    return jnp.moveaxis(y, 0, n - 1).reshape(x.shape)


def per_device(
    tokens,
    segments,
    routes,
    out_grad,
    w_query,
    w_key,
    w_value,
    w_out,
    router,
    attn_gain,
    q_gain,
    k_gain,
    ffn_gain,
    expert_gate_up,
    expert_down,
):
    F, S = lax.axis_size("fsdp"), lax.axis_size("seq")
    N = F * S
    experts = N // SPLIT
    R, D = tokens.shape
    HW = D // HEADS
    HL = HEADS // S
    CW = HL * HW
    RW = w_query.shape[0]
    L = S * R
    scale = HW ** (-0.5)
    me_f, me_s = lax.axis_index("fsdp"), lax.axis_index("seq")
    me = me_f * S + me_s
    order = mask_order(S)
    slots = jnp.stack([me_s ^ m for m in order + [m | 1 for m in order]])

    def shift_in(x, j):
        return lax.ppermute(x, "fsdp", [((i + j) % F, i) for i in range(F)])

    def shift_back(x, j):
        return lax.ppermute(x, "fsdp", [(i, (i + j) % F) for i in range(F)])

    def in_order(pieces):
        return [a for m in order for a in pieces[m]]

    def sequence_rows(x):
        mine = gather_pieces(x, S)
        return jnp.concatenate(in_order(mine) + in_order(other_core(mine, S)))

    w_low = jnp.stack([w.astype(BF16) for w in (w_query, w_key, w_value)], axis=1)
    w_send = w_low.reshape(RW, 3, S, CW).transpose(2, 0, 1, 3).reshape(S, RW, 3 * CW)
    w_mine = lax.all_to_all(w_send, "seq", split_axis=0, concat_axis=0, tiled=True)
    w_mine = w_mine.reshape(S * RW, 3 * CW)
    gains = jnp.stack([attn_gain, q_gain, k_gain, ffn_gain])
    small = [gains.astype(BF16), router.T.astype(BF16), segments.astype(BF16)]
    sizes = [4 * RW, experts * RW, R]
    pad = jnp.zeros((-sum(sizes) % 128,), BF16)
    small = jnp.concatenate([a.reshape(-1) for a in small] + [pad]).reshape(1, -1, 128)
    small = after(small, w_mine)
    small = jnp.broadcast_to(small, (N,) + small.shape[1:])
    small = lax.all_to_all(small, BOTH, split_axis=0, concat_axis=0, tiled=True).reshape(N, -1)
    parts, at = [], 0
    for n in sizes:
        parts.append(small[:, at : at + n])
        at += n
    gains_all = parts[0].reshape(N, 4, RW).transpose(1, 0, 2).reshape(4, D).astype(F32)
    ga, gq, gk, gf = [gains_all[i] for i in range(4)]
    router_t = parts[1].reshape(N, experts, RW).transpose(1, 0, 2).reshape(experts, D)
    segment_all = lax.dynamic_slice(parts[2].astype(F32), (me_f * S, 0), (S, R))

    wo_all = lax.all_gather(w_out.astype(BF16), BOTH, axis=0, tiled=True)
    c_all = lax.all_gather(after(out_grad, w_mine), BOTH, axis=0, tiled=True)
    expert = me // SPLIT
    unit = R // 2
    z_order = sorted(range(1, F), key=lambda j: (-min(j, F - j), j))
    hidden_width = expert_down.shape[1]
    gu_low = after(expert_gate_up, w_mine)[0].astype(BF16).reshape(D, 2 * hidden_width)
    down_low = after(expert_down, w_mine)[0].astype(BF16)

    up = down = w_mine
    ups, downs = [], []
    x_first = gather_first(after(tokens, w_mine), S)
    x_both = []
    for k in range(F - 1):
        up = lax.ppermute(up, "fsdp", [(i, i + 1) for i in range(F - 1)])
        down = lax.ppermute(down, "fsdp", [(i + 1, i) for i in range(F - 1)])
        ups.append(up)
        downs.append(down)
        if k == 0:
            keys = list(x_first)
            up, down, small, *got = lax.optimization_barrier(
                (up, down, small, *[x_first[m][0] for m in keys])
            )
            x_first = {m: [a] for m, a in zip(keys, got)}
            x_mine = gather_rest(x_first, S)
            x_other = other_core(x_first, S)
        elif k == 1:
            near = flat(x_other)
            far_keys = [m for m in x_mine if m not in x_first]
            far = [a for m in far_keys for a in x_mine[m]]
            up, down, *got = lax.optimization_barrier((up, down, *far, *near))
            far, near = got[: len(far)], got[len(far) :]
            x_other = {m: [a] for m, a in zip(keys, near)}
            for i, m in enumerate(far_keys):
                x_mine[m] = far[2 * i : 2 * i + 2]
                x_other[m] = [exchange(a, 1, S) for a in x_mine[m]]
        else:
            up, down = lax.optimization_barrier((up, down))
    x_seq = jnp.concatenate(in_order(x_mine) + in_order(x_other)).astype(F32)
    x_inverse = inverse_rms(x_seq)
    a_seq = after((x_seq * x_inverse * ga).astype(BF16), gu_low, down_low)
    cols = 3 * CW
    w_cols = jnp.concatenate(ups[::-1] + [w_mine] + downs)
    w_cols = lax.dynamic_slice(w_cols, ((F - 1 - me_f) * S * RW, 0), (D, cols))
    qkv = times(a_seq, w_cols)
    q_proj, k_proj = qkv[:, :CW], qkv[:, CW : 2 * CW]
    value = qkv[:, 2 * CW :].astype(BF16)

    def seq_sum(stats):
        stats = stats.reshape(-1, 2, S // 2, R)
        total = stats + exchange(stats, 1, S)[:, ::-1]
        for b in link_bits(S):
            other = exchange(total, b, S)
            total = total + jnp.stack([other[:, :, order.index(m ^ b)] for m in order], axis=2)
        return total.reshape(-1, L)

    squares = seq_sum(jnp.stack([jnp.sum(q_proj * q_proj, 1), jnp.sum(k_proj * k_proj, 1)]))
    inverse = lax.rsqrt(squares / D + EPSILON)
    q_inv, k_inv = inverse[0][:, None], inverse[1][:, None]
    gq_mine = lax.dynamic_slice(gq, (me_s * CW,), (CW,))
    gk_mine = lax.dynamic_slice(gk, (me_s * CW,), (CW,))
    positions = (slots[:, None] * R + jnp.arange(R, dtype=jnp.int32)[None]).reshape(L)
    segment_seq = to_slots(segment_all, S, me_s).reshape(L)
    tables = rope_tables(positions, HW)
    query = rope(q_proj * q_inv * gq_mine, tables, HL).astype(BF16)
    key = rope(k_proj * k_inv * gk_mine, tables, HL).astype(BF16)

    allowed = (positions[None, :] <= positions[:, None]) & (
        segment_seq[None, :] == segment_seq[:, None]
    )
    q_heads = query.reshape(L, HL, HW)
    k_heads = key.reshape(L, HL, HW)
    v_heads = value.reshape(L, HL, HW)
    scores = jnp.einsum("thd,uhd->htu", q_heads, k_heads, preferred_element_type=F32)
    scores = jnp.where(allowed[None], scores * scale, -1e30)
    row_max = jnp.max(scores, axis=-1, keepdims=True)
    terms = jnp.where(allowed[None], jnp.exp(scores - row_max), 0.0)
    probs = terms / jnp.sum(terms, axis=-1, keepdims=True)
    probs_low = probs.astype(BF16)
    attended = jnp.einsum("htu,uhd->thd", probs_low, v_heads, preferred_element_type=F32)
    attended = attended.reshape(L, CW).astype(BF16)
    o_send = attended.reshape(S, R, CW)
    o_send = from_slots(o_send, S, me_s)
    o_mine = lax.all_to_all(o_send, "seq", split_axis=0, concat_axis=0, tiled=True)
    o_mine = o_mine.transpose(1, 0, 2).reshape(R, D)
    middle = tokens.astype(F32) + times(o_mine, wo_all)
    mid_inv = inverse_rms(middle)
    mixed = (middle * mid_inv * gf).astype(BF16)
    expert_probs = jax.nn.softmax(times_transposed(mixed, router_t), axis=-1)

    chosen = routes[:, :, None] == jnp.arange(experts, dtype=jnp.int32)
    named = jnp.any(chosen, axis=1).astype(F32)
    gates = jnp.repeat((expert_probs * named).T, SPLIT, axis=0)
    gates = lax.all_to_all(gates, BOTH, split_axis=0, concat_axis=0, tiled=True).reshape(F, S, R)
    b = 1
    while b < F:
        gates = jnp.where((me_f & b) != 0, jnp.roll(gates, -b, axis=0), gates)
        b *= 2
    m_far, last = {0: mixed}, mixed
    for j in z_order:
        last = shift_in(after(mixed, last), j)
        m_far[j] = last
    chunks = [0] + z_order
    first = {j: gather_first(m_far[j], S) for j in chunks}
    mine = {j: gather_one_way(first[j], S, i % 2) for i, j in enumerate(chunks)}
    mine[0] = gather_rest(first[0], S)
    both = {j: [mine[j], other_core(mine[j], S)] for j in chunks}
    last_chunk = chunks[-1]
    top_level = len(link_bits(S))
    calls = [(j, side) for j in chunks for side in ((1, 0) if j == last_chunk else (0, 1))]
    tick = {call: t for t, call in enumerate(calls)}
    before = {t: [] for t in range(len(calls) + 4)}
    for i, j in enumerate(chunks):
        early = 2 + (j == last_chunk)
        t = 2 * i
        before[max(t - 2 - early, 0)].append(m_far[j])
        before[max(t - 1 - early, 0)] += flat(first[j])
        before[max(t - early, 0)] += flat(mine[j])
        before[max(t + 1 - early, 0)] += flat(both[j][1])
    c_rows = (me_f + jnp.arange(F, dtype=jnp.int32)) % F * S
    c_rows = (c_rows[:, None] + slots[None]).reshape(F, 2, S // 2) * R
    finished, kept, dots = {}, [], {}
    gate_up_grad, down_grad = None, None

    def flush(kept, gate_up_grad, down_grad):
        ms, cs, hids, dgus = [list(a) for a in zip(*kept)]
        down_grad = down_weights(hids, cs, down_grad)
        first = gate_up_weights(ms, dgus, gate_up_grad)
        return gate_up_weights(ms, dgus, gate_up_grad, first), down_grad

    def last_flush(at, level):
        ms, cs, hids, dgus = [list(a) for a in zip(*kept)]
        if level == 1:
            hids[0] = after(hids[0], *before[at])
            done["down"] = down_weights(hids, cs, down_grad)
            return [done["down"]]
        ms[0] = after(ms[0], *before[at + 1], *before[at + 2], *before[at + 3])
        done["gate_up"] = gate_up_weights(ms, dgus, gate_up_grad)
        return [done["gate_up"]]

    done = {}
    mix_sides, dmx_sides, mix_got, mix_done = {}, {}, {}, {}
    gate_rows = jnp.stack([to_slots(gates[j], S, me_s) for j in range(F)]).reshape(F * L, 1)
    for t, (j, side) in enumerate(calls):
        m_parts = [(a, 0, a.shape[0]) for m in order for a in both[j][side][m]]
        m_parts[0] = (after(m_parts[0][0], *before[t]), *m_parts[0][1:])
        row = j * L + side * (L // 2)
        mix, dmx, dot, *saved = expert_rows(
            m_parts, c_all, c_rows[j, side], gate_rows, row, gu_low, down_low
        )
        mix_sides[j, side], dmx_sides[j, side] = mix, dmx
        dots[j, side] = dot.reshape(-1)
        kept.append(saved)
        if F > 4 and len(kept) == 8 and t + 2 < len(calls):
            gate_up_grad, down_grad = flush(kept, gate_up_grad, down_grad)
            before[t + 2] += [gate_up_grad, down_grad]
            kept = []
        if side:
            mix_got[j] = exchange(mix, 1, S)
            before[t + 3].append(mix_got[j])
        if (j, 1 - side) in dmx_sides:
            given = tick[j, 1]

            def hold(level, sums):
                before[min(given + 2 + top_level - level, len(calls) + 3)].extend(sums)
                return sums

            ties = None
            if j == last_chunk:
                ties = {n: lambda n=n: last_flush(len(calls), n) for n in (0, 1)}

            group = (dmx_sides[j, 0], exchange(dmx_sides[j, 1], 1, S), 1, 0, chunks.index(j) % 2)
            [total] = scatter_sum([group], S, R, [BF16 if j else F32], hold, ties)
            finished[j] = shift_back(total, j) if j else total
            last_sum = total
            if F > 4:
                group = (mix_sides.pop((j, 0)), mix_got.pop(j), 1, 0, chunks.index(j) % 2)
                [mix_done[j]] = scatter_sum([group], S, R, [BF16])
                before[min(t + 4, len(calls) + 3)].append(mix_done[j])
    dots = {j: jnp.concatenate([dots[j, 0], dots[j, 1]]).reshape(S, R) for j in chunks}
    if F <= 4:
        mix_groups = [(mix_sides[j, 0], mix_got[j], 1, 0, i % 2) for i, j in enumerate(chunks)]
    dots = [dots[j] for j in range(F)]
    finished = [finished[j] for j in range(F)]
    dmx_total = finished[0]
    for t in finished[1:]:
        dmx_total = dmx_total + t.astype(F32)
    ms, _, _, dgus = [list(a) for a in zip(*kept)]
    ms[0] = after(ms[0], last_sum)
    gate_up_grad = gate_up_weights(ms, dgus, gate_up_grad, done["gate_up"])
    down_grad = done["down"]
    dmx_total = after(dmx_total, gate_up_grad)
    expert_gate_up_grad, expert_down_grad = gate_up_grad[None], down_grad[None]
    dots = jnp.stack([from_slots(d, S, me_s) for d in dots])
    b = 1
    while b < F:
        dots = jnp.where((me_f & b) != 0, jnp.roll(dots, b, axis=0), dots)
        b *= 2
    dots = dots.reshape(N, R)
    dots = lax.all_to_all(dots, BOTH, split_axis=0, concat_axis=0, tiled=True)
    grad_probs = jnp.sum(dots.reshape(experts, SPLIT, R), axis=1).T * named
    grad_logits = expert_probs * (
        grad_probs - jnp.sum(expert_probs * grad_probs, axis=-1, keepdims=True)
    )
    grad_logits = grad_logits.astype(BF16)
    router_part = rows_by_rows(grad_logits, mixed)
    grad_mixed = dmx_total + times(grad_logits, router_t)

    grad_output = out_grad.astype(F32)
    scaled = grad_mixed * gf
    grad_middle = (
        grad_output
        + mid_inv * scaled
        - middle * mid_inv**3 * jnp.mean(scaled * middle, axis=-1, keepdims=True)
    )
    ffn_part = jnp.sum(grad_mixed * middle * mid_inv, axis=0)
    early = jnp.concatenate([router_part, ffn_part[None]]).reshape(experts + 1, N, RW)
    early = lax.all_to_all(early.transpose(1, 0, 2), BOTH, split_axis=0, concat_axis=0, tiled=True)
    early = jnp.sum(early, axis=0)
    router_grad = early[:experts].T
    ffn_grad = early[experts]

    proj_low = grad_middle.astype(BF16)
    grad_proj = sequence_rows(proj_low)
    out_part = rows_by_rows(attended, grad_proj).astype(BF16).reshape(F, RW, D)
    out_grad_total = None
    for d in range(F):
        chunk = lax.dynamic_index_in_dim(out_part, (me_f + d) % F, 0, keepdims=False)
        pairs = [(f * S + s, F * s + (f + d) % F) for f in range(F) for s in range(S)]
        got = lax.ppermute(chunk, BOTH, pairs).astype(F32)
        out_grad_total = got if d == 0 else out_grad_total + got
    def hold_mix(level, sums):
        return [after(a, grad_proj) for a in sums] if level == 1 else sums

    output = middle
    if F <= 4:
        mix_done = dict(zip(chunks, scatter_sum(mix_groups, S, R, [BF16] * F, hold_mix)))
    for j in chunks:
        output = output + (shift_back(mix_done[j], j) if j else mix_done[j]).astype(F32)
    output = output.astype(BF16)

    wo_rows = lax.dynamic_slice(wo_all, (me_s * CW, 0), (CW, D))
    grad_heads = times_transposed(after(grad_proj, out_part), wo_rows).astype(BF16).reshape(L, HL, HW)
    grad_p = jnp.einsum("thd,uhd->htu", grad_heads, v_heads, preferred_element_type=F32)
    delta = jnp.sum(probs * grad_p, axis=-1, keepdims=True)
    grad_s = (probs * (grad_p - delta)).astype(BF16)
    dq = jnp.einsum("htu,uhd->thd", grad_s, k_heads, preferred_element_type=F32)
    dk = jnp.einsum("htu,thd->uhd", grad_s, q_heads, preferred_element_type=F32)
    dv = jnp.einsum("htu,thd->uhd", probs_low, grad_heads, preferred_element_type=F32)
    dq = rope_back(dq.reshape(L, CW) * scale, tables, HL)
    dk = rope_back(dk.reshape(L, CW) * scale, tables, HL)
    q_part = jnp.sum(dq * q_proj * q_inv, axis=0)
    k_part = jnp.sum(dk * k_proj * k_inv, axis=0)
    dq = dq * gq_mine
    dk = dk * gk_mine
    means = jnp.stack([jnp.sum(dq * q_proj, 1), jnp.sum(dk * k_proj, 1)])
    means = seq_sum(after(means, out_grad_total)) / D
    dqp = q_inv * dq - q_proj * q_inv**3 * means[0][:, None]
    dkp = k_inv * dk - k_proj * k_inv**3 * means[1][:, None]
    dv_low = dv.reshape(L, CW).astype(BF16)
    dqk = jnp.concatenate([dqp.astype(BF16), dkp.astype(BF16)], axis=1)
    dqk = after(dqk, *mix_done.values())
    dqkv = jnp.concatenate([dqk, dv_low], axis=1)
    x_scaled = x_seq * x_inverse
    da_keep = times_transposed(dqkv[: L // 2], w_cols)
    da_give = times_transposed(dqkv[L // 2 :], w_cols)
    attn_part = jnp.sum(da_keep * x_scaled[: L // 2], axis=0) + jnp.sum(
        da_give * x_scaled[L // 2 :], axis=0
    )
    da_keep = da_keep.astype(BF16)
    da_got = exchange(da_give.astype(BF16), 1, S)
    da_mine = jnp.concatenate(
        scatter_sum([(da_keep, da_got, 2, h, h) for h in range(2)], S, unit, [F32] * 2)
    )
    w_sums = []
    for part, n in ((dv_low, 1), (dqk, 2)):
        w_part = rows_by_rows(a_seq, part).astype(BF16).reshape(N, RW, n * CW)
        w_got = lax.all_to_all(w_part, BOTH, split_axis=0, concat_axis=0, tiled=True)
        w_sum = jnp.sum(w_got.reshape(F, S, RW, n, CW).astype(F32), axis=0)
        w_sums.append(w_sum.transpose(2, 1, 0, 3).reshape(n, RW, D))
    w_sum = [w_sums[1][0], w_sums[1][1], w_sums[0][0]]
    late = jnp.stack(
        [
            attn_part,
            lax.dynamic_update_slice(jnp.zeros((D,), F32), q_part, (me_s * CW,)),
            lax.dynamic_update_slice(jnp.zeros((D,), F32), k_part, (me_s * CW,)),
        ]
    )
    late = late.reshape(3, N, RW).transpose(1, 0, 2)
    late = lax.all_to_all(late, BOTH, split_axis=0, concat_axis=0, tiled=True)
    late = jnp.sum(late, axis=0)

    x = tokens.astype(F32)
    x_inv = inverse_rms(x)
    scaled = da_mine * ga
    grad_in = (
        grad_middle
        + x_inv * scaled
        - x * x_inv**3 * jnp.mean(scaled * x, axis=-1, keepdims=True)
    )
    return (
        output,
        grad_in.astype(BF16),
        w_sum[0],
        w_sum[1],
        w_sum[2],
        out_grad_total,
        router_grad,
        late[0],
        late[1],
        late[2],
        ffn_grad,
        expert_gate_up_grad,
        expert_down_grad,
    )


def solution(mesh):
    one, two = P(BOTH), P(BOTH, None)
    three, four = P(BOTH, None, None), P(BOTH, None, None, None)
    return jax.shard_map(
        per_device,
        mesh=mesh,
        in_specs=(two, one, two, two, two, two, two, two, two, one, one, one, one, four, three),
        out_specs=(two, two, two, two, two, two, two, one, one, one, one, four, three),
        check_vma=False,
    )
```

```python
import jax
import jax.numpy as jnp
from jax import lax
from jax.experimental import pallas as pl
from jax.experimental.pallas import tpu as pltpu
from jax.sharding import PartitionSpec as P

HEADS = 16
SPLIT = 2
EPSILON = 1e-05
THETA = 10000.0
BOTH = ("fsdp", "seq")
BF16 = jnp.bfloat16
F32 = jnp.float32


def rows_by_rows(left, right):
    return lax.dot_general(left, right, (((0,), (0,)), ((), ())), preferred_element_type=F32)


def times_transposed(left, right):
    return lax.dot_general(left, right, (((1,), (1,)), ((), ())), preferred_element_type=F32)


def times(left, right):
    return jnp.dot(left, right, preferred_element_type=F32)


def inverse_rms(values):
    return lax.rsqrt(jnp.mean(values * values, axis=-1, keepdims=True) + EPSILON)


def rope_tables(positions, head_width):
    half_width = head_width // 2
    frequency = THETA ** (-jnp.arange(half_width, dtype=F32) * 2.0 / head_width)
    angles = positions.astype(F32)[:, None] * frequency[None, :]
    return jnp.cos(angles)[:, None, :], jnp.sin(angles)[:, None, :]


def rope(values, tables, heads):
    rows, width = values.shape
    cosine, sine = tables
    shaped = values.reshape(rows, heads, width // heads)
    half = width // heads // 2
    a, b = shaped[..., :half], shaped[..., half:]
    turned = jnp.concatenate([a * cosine - b * sine, b * cosine + a * sine], axis=-1)
    return turned.reshape(rows, width)


def rope_back(values, tables, heads):
    cosine, sine = tables
    return rope(values, (cosine, -sine), heads)


def exchange(x, mask, size):
    return lax.ppermute(x, "seq", [(i, i ^ mask) for i in range(size)])


def link_bits(size):
    bits, b = [], 2
    while b < size:
        bits.append(b)
        b *= 2
    return bits


def mask_order(size):
    masks = [0]
    for b in link_bits(size):
        masks = masks + [m | b for m in masks]
    return masks


def set_bits(mask):
    return [1 << i for i in range(mask.bit_length()) if mask >> i & 1]


def by_count(size):
    return sorted(mask_order(size), key=lambda m: (len(set_bits(m)), m))


def half_of(pieces, i):
    if len(pieces) == 2:
        return pieces[i]
    rows = pieces[0].shape[0] // 2
    return pieces[0][i * rows : (i + 1) * rows]


def gather_first(x, size):
    return {m: [x if m == 0 else exchange(x, m, size)] for m in [0] + link_bits(size)}


def gather_rest(pieces, size):
    pieces = dict(pieces)
    for m in by_count(size):
        bits = set_bits(m)
        if len(bits) > 1:
            low, high = bits[0], bits[-1]
            pieces[m] = [
                exchange(half_of(pieces[m ^ high], 0), high, size),
                exchange(half_of(pieces[m ^ low], 1), low, size),
            ]
    return pieces


def gather_one_way(pieces, size, high):
    pieces = dict(pieces)
    for m in by_count(size):
        bits = set_bits(m)
        if len(bits) > 1:
            b = bits[-1] if high else bits[0]
            pieces[m] = [exchange(pieces[m ^ b][0], b, size)]
    return pieces


def gather_pieces(x, size):
    return gather_rest(gather_first(x, size), size)


def flat(pieces):
    return [a for p in pieces.values() for a in p]


def other_core(pieces, size):
    return {m: [exchange(a, 1, size) for a in p] for m, p in pieces.items()}


def add_blocks(outputs, dtypes, unit):
    arrays, specs, index = [], [], {}
    for out in outputs:
        for terms in out:
            for array, block in terms:
                width = array.shape[1]
                index[(id(array), block)] = len(arrays)
                arrays.append(array)
                specs.append(pl.BlockSpec((unit, width), lambda i, block=block: (block, 0)))

    where = [[[index[(id(a), k)] for a, k in terms] for terms in out] for out in outputs]
    count = len(arrays)

    def kernel(*refs):
        for out_ref, blocks in zip(refs[count:], where):
            for i, terms in enumerate(blocks):
                total = refs[terms[0]][...].astype(F32)
                for t in terms[1:]:
                    total = total + refs[t][...].astype(F32)
                out_ref[i * unit : (i + 1) * unit, :] = total.astype(out_ref.dtype)

    shapes = [
        jax.ShapeDtypeStruct((len(out) * unit, width), dtype) for out, dtype in zip(outputs, dtypes)
    ]
    bytes_moved = sum(unit * width * 2 for _ in arrays) * 2
    return pl.pallas_call(
        kernel,
        grid=(1,),
        out_shape=shapes,
        in_specs=specs,
        out_specs=[pl.BlockSpec(s.shape, lambda i: (0, 0)) for s in shapes],
        compiler_params=pltpu.CompilerParams(vmem_limit_bytes=48 << 20),
        cost_estimate=pl.CostEstimate(flops=0, bytes_accessed=bytes_moved, transcendentals=0),
    )(*arrays)


def wait_first(outs, arrays):
    if arrays is None:
        return outs
    array, block = outs[0][0][-1]
    outs[0][0][-1] = (after(array, *arrays()), block)
    return outs


def scatter_sum(groups, size, unit, dtypes, hold=None, ties=None):
    ties = ties or {}
    order = by_count(size)
    at = {m: i for i, m in enumerate(mask_order(size))}
    extra = {(m, k): [] for m in order for k in range(len(groups))}

    def terms(m, k):
        keep, got, stride, offset, _ = groups[k]
        block = at[m] * stride + offset
        return [(keep, block), (got, block)] + extra[(m, k)]

    level = max(len(set_bits(m)) for m in order)
    while level > 0:
        routes = {}
        for m in order:
            bits = set_bits(m)
            if len(bits) == level:
                for k, g in enumerate(groups):
                    routes.setdefault((m, bits[-1] if g[4] else bits[0]), []).append(k)
        outs = [[terms(m, k) for k in members] for (m, _), members in routes.items()]
        outs = wait_first(outs, ties.get(level))
        sums = add_blocks(outs, [BF16] * len(outs), unit)
        if hold is not None:
            sums = hold(level, sums)
        for ((m, b), members), x in zip(routes.items(), sums):
            arrived = exchange(x, b, size)
            for i, k in enumerate(members):
                extra[(m ^ b, k)].append((arrived, i))
        level -= 1
    outs = wait_first([[terms(0, k)] for k in range(len(groups))], ties.get(0))
    sums = add_blocks(outs, dtypes, unit)
    return sums if hold is None else hold(0, sums)


def expert_rows(m_parts, c_all, c_rows, gates, row, gu, down):
    width = gu.shape[0]
    hidden = down.shape[0]
    rows = sum(n for _, _, n in m_parts)

    def inputs(parts):
        arrays = []
        for a, _, _ in parts:
            if not any(a is b for b in arrays):
                arrays.append(a)
        places, at = [], 0
        for a, first, n in parts:
            places.append(([i for i, b in enumerate(arrays) if b is a][0], first, n, at))
            at += n
        return arrays, places

    m_arrays, m_places = inputs(m_parts)
    nc = c_rows.shape[0]
    nm, each = len(m_arrays), rows // nc
    step = 256
    steps = rows // step
    small = 16

    def kernel(*refs):
        m_in = refs[:nm]
        c_in, table, gate_in, gu_in, dn_in = refs[nm : nm + 5]
        mix_out, dmx_out, dots_ref, m_out, c_out, hid_out, dgu_out = refs[nm + 5 : nm + 12]
        (m_s, c_s, gu_w, dn_w, hid_s, mix_s, dmx_s, dgu_s, g_s, q_s, gate_ref,
         m_sem, c_sem, w_sem, o_sem) = refs[nm + 12 :]

        copies_m = [
            pltpu.make_async_copy(
                m_in[k].at[pl.ds(first, n)], m_s.at[pl.ds(at, n)], m_sem.at[i]
            )
            for i, (k, first, n, at) in enumerate(m_places)
        ]
        copies_c = [
            pltpu.make_async_copy(
                c_in.at[pl.ds(pl.multiple_of(table[i], each), each)],
                c_s.at[pl.ds(i * each, each)],
                c_sem.at[i],
            )
            for i in range(nc)
        ]
        c_places = [(0, 0, each, i * each) for i in range(nc)]
        g_copy = pltpu.make_async_copy(gate_in.at[pl.ds(row, rows)], gate_ref, w_sem.at[2])
        w_gu = pltpu.make_async_copy(gu_in, gu_w, w_sem.at[0])
        w_dn = pltpu.make_async_copy(dn_in, dn_w, w_sem.at[1])
        def of_block(copies, places, b):
            return [c for c, p in zip(copies, places) if b * step <= p[3] < (b + 1) * step]

        for c in of_block(copies_m, m_places, 0):
            c.start()
        w_gu.start()
        g_copy.start()

        def sends(b):
            here = pl.ds(b * step, step)
            return [
                pltpu.make_async_copy(dmx_s.at[here], dmx_out.at[here], o_sem.at[2 * b]),
                pltpu.make_async_copy(mix_s.at[here], mix_out.at[here], o_sem.at[2 * b + 1]),
            ]

        n = 2 * steps
        whole = [
            pltpu.make_async_copy(m_s, m_out, o_sem.at[n]),
            pltpu.make_async_copy(c_s, c_out, o_sem.at[n + 1]),
            pltpu.make_async_copy(hid_s, hid_out, o_sem.at[n + 2]),
            pltpu.make_async_copy(dgu_s, dgu_out, o_sem.at[n + 3]),
        ]

        def block(b, carry):
            r = pl.ds(pl.multiple_of(b * step, step), step)
            for k in range(steps):

                @pl.when(b == k)
                def _():
                    for c in of_block(copies_m, m_places, k):
                        c.wait()
                    if k == 0:
                        w_gu.wait()
                        g_copy.wait()
                        w_dn.start()
                        for c in of_block(copies_c, c_places, 0):
                            c.start()
                    if k + 1 < steps:
                        for c in of_block(copies_m, m_places, k + 1):
                            c.start()

            g_s[...] = times(m_s[r, :], gu_w[...])
            for k in range(steps):

                @pl.when(b == k)
                def _():
                    for c in of_block(copies_c, c_places, k):
                        c.wait()
                    if k == 0:
                        w_dn.wait()
                    if k + 1 < steps:
                        for c in of_block(copies_c, c_places, k + 1):
                            c.start()
                    else:
                        whole[0].start()
                        whole[1].start()

            q_s[...] = times_transposed(c_s[r, :], dn_w[...])
            for s in range(step // small):
                here = slice(s * small, (s + 1) * small)
                out = pl.ds(pl.multiple_of(b * step + s * small, small), small)
                scale = gate_ref[out, :]
                g = g_s[here, :hidden]
                u = g_s[here, hidden:]
                q = q_s[here, :]
                sig = jax.nn.sigmoid(g)
                act = g * sig
                hid = act * u
                dots_ref[out, :] = jnp.sum(hid * q, axis=1, keepdims=True)
                hid_s[out, :] = (hid * scale).astype(BF16)
                dh = q * scale
                dgu_s[out, :hidden] = (dh * u * (sig + act * (1.0 - sig))).astype(BF16)
                dgu_s[out, hidden:] = (dh * act).astype(BF16)
            dmx_s[r, :] = times_transposed(dgu_s[r, :], gu_w[...]).astype(BF16)
            mix_s[r, :] = times(hid_s[r, :], dn_w[...]).astype(BF16)
            for k in range(steps):

                @pl.when(b == k)
                def _():
                    for c in sends(k):
                        c.start()

            return carry

        lax.fori_loop(0, steps, block, 0)
        whole[2].start()
        whole[3].start()
        for c in whole + [c for k in range(steps) for c in sends(k)]:
            c.wait()

    anywhere = pl.BlockSpec(memory_space=pl.ANY)
    vmem = pl.BlockSpec(memory_space=pltpu.VMEM)
    sds = jax.ShapeDtypeStruct
    return pl.pallas_call(
        kernel,
        out_shape=[
            sds((rows, width), BF16),
            sds((rows, width), BF16),
            sds((rows, 1), F32),
            sds((rows, width), BF16),
            sds((rows, width), BF16),
            sds((rows, hidden), BF16),
            sds((rows, 2 * hidden), BF16),
        ],
        in_specs=[anywhere] * (nm + 1)
        + [pl.BlockSpec(memory_space=pltpu.SMEM)]
        + [anywhere] * 3,
        out_specs=[anywhere] * 2 + [vmem] + [anywhere] * 4,
        scratch_shapes=[
            pltpu.VMEM((rows, width), BF16),
            pltpu.VMEM((rows, width), BF16),
            pltpu.VMEM((width, 2 * hidden), BF16),
            pltpu.VMEM((hidden, width), BF16),
            pltpu.VMEM((rows, hidden), BF16),
            pltpu.VMEM((rows, width), BF16),
            pltpu.VMEM((rows, width), BF16),
            pltpu.VMEM((rows, 2 * hidden), BF16),
            pltpu.VMEM((step, 2 * hidden), F32),
            pltpu.VMEM((step, hidden), F32),
            pltpu.VMEM((rows, 1), F32),
            pltpu.SemaphoreType.DMA((len(m_places),)),
            pltpu.SemaphoreType.DMA((nc,)),
            pltpu.SemaphoreType.DMA((3,)),
            pltpu.SemaphoreType.DMA((2 * steps + 4,)),
        ],
        compiler_params=pltpu.CompilerParams(vmem_limit_bytes=60 << 20),
        cost_estimate=pl.CostEstimate(
            flops=2 * rows * width * hidden * 6, bytes_accessed=24 << 20, transcendentals=0
        ),
    )(*m_arrays, c_all, c_rows, gates, gu, down)


def gate_up_weights(lefts, rights, before=None, rest=None):
    rows, width = lefts[0].shape
    cols = rights[0].shape[1]
    n, tile = len(lefts), 512
    steps = width // tile // 2
    skip = 0 if rest is None else steps

    def kernel(*refs):
        total = rows_by_rows(refs[0][...], refs[n][...])
        for i in range(1, n):
            total = total + rows_by_rows(refs[i][...], refs[n + i][...])
        out = refs[-1]
        for k in range(2):
            part = total[:, k * (cols // 2) : (k + 1) * (cols // 2)]
            out[:, k, :] = part if before is None else part + refs[2 * n][:, k, :]

    block = pl.BlockSpec((tile, 2, cols // 2), lambda i: (i + skip, 0, 0))
    extra = [] if before is None else [before]
    old = [] if rest is None else [rest]
    return pl.pallas_call(
        kernel,
        grid=(steps,),
        out_shape=jax.ShapeDtypeStruct((width, 2, cols // 2), F32),
        in_specs=[pl.BlockSpec((rows, tile), lambda i: (0, i + skip))] * n
        + [pl.BlockSpec((rows, cols), lambda i: (0, 0))] * n
        + [block] * len(extra)
        + [pl.BlockSpec(memory_space=pl.ANY)] * len(old),
        out_specs=block,
        input_output_aliases={2 * n + len(extra): 0} if old else {},
        compiler_params=pltpu.CompilerParams(vmem_limit_bytes=58 << 20),
        cost_estimate=pl.CostEstimate(
            flops=n * rows * width * cols, bytes_accessed=16 << 20, transcendentals=0
        ),
    )(*lefts, *rights, *extra, *old)


def down_weights(lefts, rights, before=None):
    rows, hidden = lefts[0].shape
    width = rights[0].shape[1]
    n, tile = len(lefts), 512

    def kernel(*refs):
        total = rows_by_rows(refs[0][...], refs[n][...])
        for i in range(1, n):
            total = total + rows_by_rows(refs[i][...], refs[n + i][...])
        refs[-1][...] = total if before is None else total + refs[2 * n][...]

    block = pl.BlockSpec((hidden, tile), lambda i: (0, i))
    extra = [] if before is None else [before]
    return pl.pallas_call(
        kernel,
        grid=(width // tile,),
        out_shape=jax.ShapeDtypeStruct((hidden, width), F32),
        in_specs=[pl.BlockSpec((rows, hidden), lambda i: (0, 0))] * n
        + [pl.BlockSpec((rows, tile), lambda i: (0, i))] * n
        + [block] * len(extra),
        out_specs=block,
        compiler_params=pltpu.CompilerParams(vmem_limit_bytes=58 << 20),
        cost_estimate=pl.CostEstimate(
            flops=2 * n * rows * width * hidden, bytes_accessed=24 << 20, transcendentals=0
        ),
    )(*lefts, *rights, *extra)


def after(x, *others):
    return lax.optimization_barrier((x, *others))[0]


def flip_slots(x, size, me):
    n = len(link_bits(size)) + 1
    for axis, b in enumerate([1] + link_bits(size)[::-1]):
        x = jnp.where((me & b) != 0, jnp.flip(x, axis), x)
    return x, n


def to_slots(x, size, me):
    n = len(link_bits(size)) + 1
    y = jnp.moveaxis(x.reshape((2,) * n + x.shape[1:]), n - 1, 0)
    return flip_slots(y, size, me)[0].reshape(x.shape)


def from_slots(x, size, me):
    n = len(link_bits(size)) + 1
    y = flip_slots(x.reshape((2,) * n + x.shape[1:]), size, me)[0]
    return jnp.moveaxis(y, 0, n - 1).reshape(x.shape)


def sum_to_owners(x, planes, size, plane, place):
    n, _, rows = x.shape
    for axis, count, me in (("seq", size, place), ("fsdp", planes, plane)):
        outer = planes if axis == "seq" else 1
        b = 1
        while b < count:
            y = x.reshape(n, outer, -1, 2, rows)
            high = (me & b) != 0
            mine = jnp.where(high, y[:, :, :, 1], y[:, :, :, 0])
            theirs = jnp.where(high, y[:, :, :, 0], y[:, :, :, 1])
            x = mine + lax.ppermute(theirs, axis, [(i, i ^ b) for i in range(count)])
            x = x.reshape(n, -1, rows)
            b *= 2
    return x[:, 0]


def per_device(
    tokens,
    segments,
    routes,
    out_grad,
    w_query,
    w_key,
    w_value,
    w_out,
    router,
    attn_gain,
    q_gain,
    k_gain,
    ffn_gain,
    expert_gate_up,
    expert_down,
):
    F, S = lax.axis_size("fsdp"), lax.axis_size("seq")
    N = F * S
    experts = N // SPLIT
    R, D = tokens.shape
    HW = D // HEADS
    HL = HEADS // S
    CW = HL * HW
    RW = w_query.shape[0]
    L = S * R
    scale = HW ** (-0.5)
    me_f, me_s = lax.axis_index("fsdp"), lax.axis_index("seq")
    me = me_f * S + me_s
    order = mask_order(S)
    slots = jnp.stack([me_s ^ m for m in order + [m | 1 for m in order]])

    def shift_in(x, j):
        return lax.ppermute(x, "fsdp", [((i + j) % F, i) for i in range(F)])

    def shift_back(x, j):
        return lax.ppermute(x, "fsdp", [(i, (i + j) % F) for i in range(F)])

    def in_order(pieces):
        return [a for m in order for a in pieces[m]]

    def sequence_rows(x):
        mine = gather_pieces(x, S)
        return jnp.concatenate(in_order(mine) + in_order(other_core(mine, S)))

    w_low = jnp.stack([w.astype(BF16) for w in (w_query, w_key, w_value)], axis=1)
    w_send = w_low.reshape(RW, 3, S, CW).transpose(2, 0, 1, 3).reshape(S, RW, 3 * CW)
    w_mine = lax.all_to_all(w_send, "seq", split_axis=0, concat_axis=0, tiled=True)
    w_mine = w_mine.reshape(S * RW, 3 * CW)
    wo_all = lax.all_gather(w_out.astype(BF16), BOTH, axis=0, tiled=True)
    c_all = lax.all_gather(after(out_grad, w_mine), BOTH, axis=0, tiled=True)
    expert = me // SPLIT
    unit = R // 2
    z_order = sorted(range(1, F), key=lambda j: (-min(j, F - j), j))
    hidden_width = expert_down.shape[1]
    gu_low = after(expert_gate_up, w_mine)[0].astype(BF16).reshape(D, 2 * hidden_width)
    down_low = after(expert_down, w_mine)[0].astype(BF16)

    up = down = w_mine
    ups, downs = [], []
    x_first = gather_first(after(tokens, w_mine), S)
    x_both = []
    for k in range(F - 1):
        up = lax.ppermute(up, "fsdp", [(i, i + 1) for i in range(F - 1)])
        down = lax.ppermute(down, "fsdp", [(i + 1, i) for i in range(F - 1)])
        ups.append(up)
        downs.append(down)
        if k == 0:
            keys = list(x_first)
            up, down, *got = lax.optimization_barrier(
                (up, down, *[x_first[m][0] for m in keys])
            )
            x_first = {m: [a] for m, a in zip(keys, got)}
            x_mine = gather_rest(x_first, S)
            x_other = other_core(x_first, S)
        elif k == 1:
            near = flat(x_other)
            far_keys = [m for m in x_mine if m not in x_first]
            far = [a for m in far_keys for a in x_mine[m]]
            up, down, *got = lax.optimization_barrier((up, down, *far, *near))
            far, near = got[: len(far)], got[len(far) :]
            x_other = {m: [a] for m, a in zip(keys, near)}
            for i, m in enumerate(far_keys):
                x_mine[m] = far[2 * i : 2 * i + 2]
                x_other[m] = [exchange(a, 1, S) for a in x_mine[m]]
        else:
            up, down = lax.optimization_barrier((up, down))
    x_seq = jnp.concatenate(in_order(x_mine) + in_order(x_other)).astype(F32)
    gains = jnp.stack([attn_gain, q_gain, k_gain, ffn_gain])
    small = [gains.astype(BF16), router.T.astype(BF16), segments.astype(BF16)]
    sizes = [4 * RW, experts * RW, R]
    pad = jnp.zeros((-sum(sizes) % 128,), BF16)
    small = jnp.concatenate([a.reshape(-1) for a in small] + [pad]).reshape(1, -1, 128)
    small = after(small, ups[min(1, F - 2)])
    small = jnp.broadcast_to(small, (N,) + small.shape[1:])
    small = lax.all_to_all(small, BOTH, split_axis=0, concat_axis=0, tiled=True).reshape(N, -1)
    parts, at = [], 0
    for n in sizes:
        parts.append(small[:, at : at + n])
        at += n
    gains_all = parts[0].reshape(N, 4, RW).transpose(1, 0, 2).reshape(4, D).astype(F32)
    ga, gq, gk, gf = [gains_all[i] for i in range(4)]
    router_t = parts[1].reshape(N, experts, RW).transpose(1, 0, 2).reshape(experts, D)
    segment_all = lax.dynamic_slice(parts[2].astype(F32), (me_f * S, 0), (S, R))

    x_inverse = inverse_rms(x_seq)
    a_seq = after((x_seq * x_inverse * ga).astype(BF16), gu_low, down_low)
    cols = 3 * CW
    w_cols = jnp.concatenate(ups[::-1] + [w_mine] + downs)
    w_cols = lax.dynamic_slice(w_cols, ((F - 1 - me_f) * S * RW, 0), (D, cols))
    qkv = times(a_seq, w_cols)
    q_proj, k_proj = qkv[:, :CW], qkv[:, CW : 2 * CW]
    value = qkv[:, 2 * CW :].astype(BF16)

    def seq_sum(stats):
        stats = stats.reshape(-1, 2, S // 2, R)
        total = stats + exchange(stats, 1, S)[:, ::-1]
        for b in link_bits(S):
            other = exchange(total, b, S)
            total = total + jnp.stack([other[:, :, order.index(m ^ b)] for m in order], axis=2)
        return total.reshape(-1, L)

    squares = seq_sum(jnp.stack([jnp.sum(q_proj * q_proj, 1), jnp.sum(k_proj * k_proj, 1)]))
    inverse = lax.rsqrt(squares / D + EPSILON)
    q_inv, k_inv = inverse[0][:, None], inverse[1][:, None]
    gq_mine = lax.dynamic_slice(gq, (me_s * CW,), (CW,))
    gk_mine = lax.dynamic_slice(gk, (me_s * CW,), (CW,))
    positions = (slots[:, None] * R + jnp.arange(R, dtype=jnp.int32)[None]).reshape(L)
    segment_seq = to_slots(segment_all, S, me_s).reshape(L)
    tables = rope_tables(positions, HW)
    query = rope(q_proj * q_inv * gq_mine, tables, HL).astype(BF16)
    key = rope(k_proj * k_inv * gk_mine, tables, HL).astype(BF16)

    allowed = (positions[None, :] <= positions[:, None]) & (
        segment_seq[None, :] == segment_seq[:, None]
    )
    q_heads = query.reshape(L, HL, HW)
    k_heads = key.reshape(L, HL, HW)
    v_heads = value.reshape(L, HL, HW)
    scores = jnp.einsum("thd,uhd->htu", q_heads, k_heads, preferred_element_type=F32)
    scores = jnp.where(allowed[None], scores * scale, -1e30)
    row_max = jnp.max(scores, axis=-1, keepdims=True)
    terms = jnp.where(allowed[None], jnp.exp(scores - row_max), 0.0)
    probs = terms / jnp.sum(terms, axis=-1, keepdims=True)
    probs_low = probs.astype(BF16)
    attended = jnp.einsum("htu,uhd->thd", probs_low, v_heads, preferred_element_type=F32)
    attended = attended.reshape(L, CW).astype(BF16)
    o_send = attended.reshape(S, R, CW)
    o_send = from_slots(o_send, S, me_s)
    o_mine = lax.all_to_all(o_send, "seq", split_axis=0, concat_axis=0, tiled=True)
    o_mine = o_mine.transpose(1, 0, 2).reshape(R, D)
    middle = tokens.astype(F32) + times(o_mine, wo_all)
    mid_inv = inverse_rms(middle)
    mixed = (middle * mid_inv * gf).astype(BF16)
    expert_probs = jax.nn.softmax(times_transposed(mixed, router_t), axis=-1)

    chosen = routes[:, :, None] == jnp.arange(experts, dtype=jnp.int32)
    named = jnp.any(chosen, axis=1).astype(F32)
    gates = jnp.repeat((expert_probs * named).T, SPLIT, axis=0)
    gates = lax.all_to_all(gates, BOTH, split_axis=0, concat_axis=0, tiled=True).reshape(F, S, R)
    b = 1
    while b < F:
        gates = jnp.where((me_f & b) != 0, jnp.roll(gates, -b, axis=0), gates)
        b *= 2
    m_far, last = {0: mixed}, mixed
    for j in z_order:
        last = shift_in(after(mixed, last), j)
        m_far[j] = last
    chunks = [0] + z_order
    first = {j: gather_first(m_far[j], S) for j in chunks}
    mine = {j: gather_one_way(first[j], S, i % 2) for i, j in enumerate(chunks)}
    mine[0] = gather_rest(first[0], S)
    both = {j: [mine[j], other_core(mine[j], S)] for j in chunks}
    last_chunk = chunks[-1]
    top_level = len(link_bits(S))
    calls = [(j, side) for j in chunks for side in ((1, 0) if j == last_chunk else (0, 1))]
    tick = {call: t for t, call in enumerate(calls)}
    before = {t: [] for t in range(len(calls) + 4)}
    for i, j in enumerate(chunks):
        early = 1 if j == last_chunk else 0
        t = 2 * i
        before[max(t - 2 - early, 0)].append(m_far[j])
        before[max(t - 1 - early, 0)] += flat(first[j])
        before[max(t - early, 0)] += flat(mine[j])
        before[max(t + 1 - early, 0)] += flat(both[j][1])
    c_rows = (me_f + jnp.arange(F, dtype=jnp.int32)) % F * S
    c_rows = (c_rows[:, None] + slots[None]).reshape(F, 2, S // 2) * R
    finished, kept, dots = {}, [], {}
    gate_up_grad, down_grad = None, None

    def flush(kept, gate_up_grad, down_grad):
        ms, cs, hids, dgus = [list(a) for a in zip(*kept)]
        down_grad = down_weights(hids, cs, down_grad)
        first = gate_up_weights(ms, dgus, gate_up_grad)
        return gate_up_weights(ms, dgus, gate_up_grad, first), down_grad

    def last_flush(at, level):
        ms, cs, hids, dgus = [list(a) for a in zip(*kept)]
        if level == 1:
            hids[0] = after(hids[0], *before[at])
            done["down"] = down_weights(hids, cs, down_grad)
            return [done["down"]]
        ms[0] = after(ms[0], *before[at + 1], *before[at + 2], *before[at + 3])
        done["gate_up"] = gate_up_weights(ms, dgus, gate_up_grad)
        return [done["gate_up"]]

    done = {}
    mix_sides, dmx_sides, mix_got, mix_done = {}, {}, {}, {}
    gate_rows = jnp.stack([to_slots(gates[j], S, me_s) for j in range(F)]).reshape(F * L, 1)
    for t, (j, side) in enumerate(calls):
        m_parts = [(a, 0, a.shape[0]) for m in order for a in both[j][side][m]]
        m_parts[0] = (after(m_parts[0][0], *before[t]), *m_parts[0][1:])
        row = j * L + side * (L // 2)
        mix, dmx, dot, *saved = expert_rows(
            m_parts, c_all, c_rows[j, side], gate_rows, row, gu_low, down_low
        )
        mix_sides[j, side], dmx_sides[j, side] = mix, dmx
        dots[j, side] = dot.reshape(-1)
        kept.append(saved)
        if F > 4 and len(kept) == 8 and t + 2 < len(calls):
            gate_up_grad, down_grad = flush(kept, gate_up_grad, down_grad)
            before[t + 2] += [gate_up_grad, down_grad]
            kept = []
        if side:
            mix_got[j] = exchange(mix, 1, S)
            before[t + 3].append(mix_got[j])
        if (j, 1 - side) in dmx_sides:
            given = tick[j, 1]

            def hold(level, sums):
                before[min(given + 2 + top_level - level, len(calls) + 3)].extend(sums)
                return sums

            ties = None
            if j == last_chunk:
                ties = {n: lambda n=n: last_flush(len(calls), n) for n in (0, 1)}

            way = chunks.index(j) % 2
            both_sums = [(dmx_sides[j, 0], exchange(dmx_sides[j, 1], 1, S), 1, 0, way)]
            both_sums.append((mix_sides.pop((j, 0)), mix_got.pop(j), 1, 0, 1 - way))
            total, mix = scatter_sum(both_sums, S, R, [BF16 if j else F32, BF16], hold, ties)
            mix_done[j] = shift_back(mix, j) if j else mix
            before[min(given + 5, len(calls) + 3)].append(mix_done[j])
            finished[j] = shift_back(total, j) if j else total
            last_sum = total
    dots = {j: jnp.concatenate([dots[j, 0], dots[j, 1]]).reshape(S, R) for j in chunks}
    dots = [dots[j] for j in range(F)]
    finished = [finished[j] for j in range(F)]
    dmx_total = finished[0]
    for t in finished[1:]:
        dmx_total = dmx_total + t.astype(F32)
    ms, _, _, dgus = [list(a) for a in zip(*kept)]
    ms[0] = after(ms[0], last_sum)
    gate_up_grad = gate_up_weights(ms, dgus, gate_up_grad, done["gate_up"])
    down_grad = done["down"]
    dmx_total = after(dmx_total, gate_up_grad)
    expert_gate_up_grad, expert_down_grad = gate_up_grad[None], down_grad[None]
    dots = jnp.stack([from_slots(d, S, me_s) for d in dots])
    b = 1
    while b < F:
        dots = jnp.where((me_f & b) != 0, jnp.roll(dots, b, axis=0), dots)
        b *= 2
    dots = dots.reshape(N, R)
    dots = lax.all_to_all(dots, BOTH, split_axis=0, concat_axis=0, tiled=True)
    dots = after(dots, gate_up_grad)
    grad_probs = jnp.sum(dots.reshape(experts, SPLIT, R), axis=1).T * named
    grad_logits = expert_probs * (
        grad_probs - jnp.sum(expert_probs * grad_probs, axis=-1, keepdims=True)
    )
    grad_logits = grad_logits.astype(BF16)
    router_part = rows_by_rows(grad_logits, mixed)
    grad_mixed = dmx_total + times(grad_logits, router_t)

    grad_output = out_grad.astype(F32)
    scaled = grad_mixed * gf
    grad_middle = (
        grad_output
        + mid_inv * scaled
        - middle * mid_inv**3 * jnp.mean(scaled * middle, axis=-1, keepdims=True)
    )
    ffn_part = jnp.sum(grad_mixed * middle * mid_inv, axis=0)
    early = jnp.concatenate([router_part, ffn_part[None]]).reshape(experts + 1, N, RW)
    early = sum_to_owners(early, F, S, me_f, me_s)
    router_grad = early[:experts].T
    ffn_grad = early[experts]

    proj_low = grad_middle.astype(BF16)
    grad_proj = sequence_rows(proj_low)
    out_part = rows_by_rows(attended, grad_proj).astype(BF16)
    out_sum = lax.psum_scatter(out_part, "fsdp", scatter_dimension=0, tiled=True)
    pairs = [(f * S + s, F * s + f) for f in range(F) for s in range(S)]
    out_grad_total = lax.ppermute(out_sum, BOTH, pairs).astype(F32)
    output = middle
    for j in chunks:
        output = output + mix_done[j].astype(F32)
    output = output.astype(BF16)

    wo_rows = lax.dynamic_slice(wo_all, (me_s * CW, 0), (CW, D))
    grad_heads = times_transposed(after(grad_proj, out_part, early, *mix_done.values()), wo_rows).astype(BF16).reshape(L, HL, HW)
    grad_p = jnp.einsum("thd,uhd->htu", grad_heads, v_heads, preferred_element_type=F32)
    delta = jnp.sum(probs * grad_p, axis=-1, keepdims=True)
    grad_s = (probs * (grad_p - delta)).astype(BF16)
    dq = jnp.einsum("htu,uhd->thd", grad_s, k_heads, preferred_element_type=F32)
    dk = jnp.einsum("htu,thd->uhd", grad_s, q_heads, preferred_element_type=F32)
    dv = jnp.einsum("htu,thd->uhd", probs_low, grad_heads, preferred_element_type=F32)
    dq = rope_back(dq.reshape(L, CW) * scale, tables, HL)
    dk = rope_back(dk.reshape(L, CW) * scale, tables, HL)
    q_part = jnp.sum(dq * q_proj * q_inv, axis=0)
    k_part = jnp.sum(dk * k_proj * k_inv, axis=0)
    dq = dq * gq_mine
    dk = dk * gk_mine
    means = jnp.stack([jnp.sum(dq * q_proj, 1), jnp.sum(dk * k_proj, 1)])
    means = seq_sum(means) / D
    dqp = q_inv * dq - q_proj * q_inv**3 * means[0][:, None]
    dkp = k_inv * dk - k_proj * k_inv**3 * means[1][:, None]
    dv_low = dv.reshape(L, CW).astype(BF16)
    dqk = jnp.concatenate([dqp.astype(BF16), dkp.astype(BF16)], axis=1)
    v_part = rows_by_rows(a_seq, dv_low).astype(BF16)
    v_sum = lax.psum_scatter(v_part, "fsdp", scatter_dimension=0, tiled=True)
    qk_part = rows_by_rows(a_seq, dqk).astype(BF16).reshape(N, RW, 2 * CW)
    qk_got = lax.all_to_all(qk_part, BOTH, split_axis=0, concat_axis=0, tiled=True)
    qk_parts = qk_got.reshape(F, S, RW, 2 * CW)
    qk_all = qk_parts[0].astype(F32)
    for f in range(1, F):
        qk_all = qk_all + qk_parts[f].astype(F32)
    qk_sum = [
        qk_all[:, :, i * CW : (i + 1) * CW].transpose(1, 0, 2).reshape(RW, D) for i in range(2)
    ]
    v_got = lax.all_to_all(
        after(v_sum, qk_got).reshape(S, RW, CW), "seq", split_axis=0, concat_axis=0, tiled=True
    )
    w_sum = [qk_sum[0], qk_sum[1], v_got.transpose(1, 0, 2).reshape(RW, D).astype(F32)]
    dqkv = jnp.concatenate([after(dqk, qk_part), dv_low], axis=1)
    x_scaled = x_seq * x_inverse
    da_keep = times_transposed(dqkv[: L // 2], w_cols)
    da_give = times_transposed(dqkv[L // 2 :], w_cols)
    attn_part = jnp.sum(da_keep * x_scaled[: L // 2], axis=0) + jnp.sum(
        da_give * x_scaled[L // 2 :], axis=0
    )
    da_keep = da_keep.astype(BF16)
    da_got = exchange(da_give.astype(BF16), 1, S)
    da_mine = jnp.concatenate(
        scatter_sum([(da_keep, da_got, 2, h, h) for h in range(2)], S, unit, [F32] * 2)
    )
    late = jnp.stack(
        [
            attn_part,
            lax.dynamic_update_slice(jnp.zeros((D,), F32), q_part, (me_s * CW,)),
            lax.dynamic_update_slice(jnp.zeros((D,), F32), k_part, (me_s * CW,)),
        ]
    )
    late = late.reshape(3, N, RW).transpose(1, 0, 2)
    late = lax.all_to_all(late, BOTH, split_axis=0, concat_axis=0, tiled=True)
    late = jnp.sum(late, axis=0)

    x = tokens.astype(F32)
    x_inv = inverse_rms(x)
    scaled = da_mine * ga
    grad_in = (
        grad_middle
        + x_inv * scaled
        - x * x_inv**3 * jnp.mean(scaled * x, axis=-1, keepdims=True)
    )
    return (
        output,
        grad_in.astype(BF16),
        w_sum[0],
        w_sum[1],
        w_sum[2],
        out_grad_total,
        router_grad,
        late[0],
        late[1],
        late[2],
        ffn_grad,
        expert_gate_up_grad,
        expert_down_grad,
    )


def solution(mesh):
    one, two = P(BOTH), P(BOTH, None)
    three, four = P(BOTH, None, None), P(BOTH, None, None, None)
    return jax.shard_map(
        per_device,
        mesh=mesh,
        in_specs=(two, one, two, two, two, two, two, two, two, one, one, one, one, four, three),
        out_specs=(two, two, two, two, two, two, two, one, one, one, one, four, three),
        check_vma=False,
    )
```

```python
import jax
import jax.numpy as jnp
from jax import lax
from jax.experimental import pallas as pl
from jax.experimental.pallas import tpu as pltpu
from jax.sharding import PartitionSpec as P

HEADS = 16
SPLIT = 2
EPSILON = 1e-05
THETA = 10000.0
BOTH = ("fsdp", "seq")
BF16 = jnp.bfloat16
F32 = jnp.float32


def rows_by_rows(left, right):
    return lax.dot_general(left, right, (((0,), (0,)), ((), ())), preferred_element_type=F32)


def times_transposed(left, right):
    return lax.dot_general(left, right, (((1,), (1,)), ((), ())), preferred_element_type=F32)


def times(left, right):
    return jnp.dot(left, right, preferred_element_type=F32)


def inverse_rms(values):
    return lax.rsqrt(jnp.mean(values * values, axis=-1, keepdims=True) + EPSILON)


def rope_tables(positions, head_width):
    half_width = head_width // 2
    frequency = THETA ** (-jnp.arange(half_width, dtype=F32) * 2.0 / head_width)
    angles = positions.astype(F32)[:, None] * frequency[None, :]
    return jnp.cos(angles)[:, None, :], jnp.sin(angles)[:, None, :]


def exchange(x, mask, size):
    return lax.ppermute(x, "seq", [(i, i ^ mask) for i in range(size)])


def link_bits(size):
    bits, b = [], 2
    while b < size:
        bits.append(b)
        b *= 2
    return bits


def mask_order(size):
    masks = [0]
    for b in link_bits(size):
        masks = masks + [m | b for m in masks]
    return masks


def set_bits(mask):
    return [1 << i for i in range(mask.bit_length()) if mask >> i & 1]


def by_count(size):
    return sorted(mask_order(size), key=lambda m: (len(set_bits(m)), m))


def half_of(pieces, i):
    if len(pieces) == 2:
        return pieces[i]
    rows = pieces[0].shape[0] // 2
    return pieces[0][i * rows : (i + 1) * rows]


def gather_first(x, size):
    return {m: [x if m == 0 else exchange(x, m, size)] for m in [0] + link_bits(size)}


def gather_rest(pieces, size):
    pieces = dict(pieces)
    for m in by_count(size):
        bits = set_bits(m)
        if len(bits) > 1:
            low, high = bits[0], bits[-1]
            pieces[m] = [
                exchange(half_of(pieces[m ^ high], 0), high, size),
                exchange(half_of(pieces[m ^ low], 1), low, size),
            ]
    return pieces


def gather_one_way(pieces, size, high):
    pieces = dict(pieces)
    for m in by_count(size):
        bits = set_bits(m)
        if len(bits) > 1:
            b = bits[-1] if high else bits[0]
            pieces[m] = [exchange(pieces[m ^ b][0], b, size)]
    return pieces


def gather_pieces(x, size):
    return gather_rest(gather_first(x, size), size)


def flat(pieces):
    return [a for p in pieces.values() for a in p]


def other_core(pieces, size):
    return {m: [exchange(a, 1, size) for a in p] for m, p in pieces.items()}


def add_blocks(outputs, dtypes, unit):
    arrays, specs, index = [], [], {}
    for out in outputs:
        for terms in out:
            for array, block in terms:
                width = array.shape[1]
                index[(id(array), block)] = len(arrays)
                arrays.append(array)
                specs.append(pl.BlockSpec((unit, width), lambda i, block=block: (block, 0)))

    where = [[[index[(id(a), k)] for a, k in terms] for terms in out] for out in outputs]
    count = len(arrays)

    def kernel(*refs):
        for out_ref, blocks in zip(refs[count:], where):
            for i, terms in enumerate(blocks):
                total = refs[terms[0]][...].astype(F32)
                for t in terms[1:]:
                    total = total + refs[t][...].astype(F32)
                out_ref[i * unit : (i + 1) * unit, :] = total.astype(out_ref.dtype)

    shapes = [
        jax.ShapeDtypeStruct((len(out) * unit, width), dtype) for out, dtype in zip(outputs, dtypes)
    ]
    bytes_moved = sum(unit * width * 2 for _ in arrays) * 2
    return pl.pallas_call(
        kernel,
        grid=(1,),
        out_shape=shapes,
        in_specs=specs,
        out_specs=[pl.BlockSpec(s.shape, lambda i: (0, 0)) for s in shapes],
        compiler_params=pltpu.CompilerParams(vmem_limit_bytes=48 << 20),
        cost_estimate=pl.CostEstimate(flops=0, bytes_accessed=bytes_moved, transcendentals=0),
    )(*arrays)


def wait_first(outs, arrays):
    if arrays is None:
        return outs
    array, block = outs[0][0][-1]
    outs[0][0][-1] = (after(array, *arrays()), block)
    return outs


def scatter_sum(groups, size, unit, dtypes, hold=None, ties=None):
    ties = ties or {}
    order = by_count(size)
    at = {m: i for i, m in enumerate(mask_order(size))}
    extra = {(m, k): [] for m in order for k in range(len(groups))}

    def terms(m, k):
        keep, got, stride, offset, _ = groups[k]
        block = at[m] * stride + offset
        return [(keep, block), (got, block)] + extra[(m, k)]

    level = max(len(set_bits(m)) for m in order)
    while level > 0:
        routes = {}
        for m in order:
            bits = set_bits(m)
            if len(bits) == level:
                for k, g in enumerate(groups):
                    routes.setdefault((m, bits[-1] if g[4] else bits[0]), []).append(k)
        outs = [[terms(m, k) for k in members] for (m, _), members in routes.items()]
        outs = wait_first(outs, ties.get(level))
        sums = add_blocks(outs, [BF16] * len(outs), unit)
        if hold is not None:
            sums = hold(level, sums)
        for ((m, b), members), x in zip(routes.items(), sums):
            arrived = exchange(x, b, size)
            for i, k in enumerate(members):
                extra[(m ^ b, k)].append((arrived, i))
        level -= 1
    outs = wait_first([[terms(0, k)] for k in range(len(groups))], ties.get(0))
    sums = add_blocks(outs, dtypes, unit)
    return sums if hold is None else hold(0, sums)


def expert_rows(m_parts, c_all, c_rows, gates, row, gu, down):
    width = gu.shape[0]
    hidden = down.shape[0]
    rows = sum(n for _, _, n in m_parts)

    def inputs(parts):
        arrays = []
        for a, _, _ in parts:
            if not any(a is b for b in arrays):
                arrays.append(a)
        places, at = [], 0
        for a, first, n in parts:
            places.append(([i for i, b in enumerate(arrays) if b is a][0], first, n, at))
            at += n
        return arrays, places

    m_arrays, m_places = inputs(m_parts)
    nc = c_rows.shape[0]
    nm, each = len(m_arrays), rows // nc
    step = 256
    steps = rows // step
    small = 16

    def kernel(*refs):
        m_in = refs[:nm]
        c_in, table, gate_in, gu_in, dn_in = refs[nm : nm + 5]
        mix_out, dmx_out, dots_ref, m_out, c_out, hid_out, dgu_out = refs[nm + 5 : nm + 12]
        (m_s, c_s, gu_w, dn_w, hid_s, mix_s, dmx_s, dgu_s, g_s, q_s, gate_ref,
         m_sem, c_sem, w_sem, o_sem) = refs[nm + 12 :]

        copies_m = [
            pltpu.make_async_copy(
                m_in[k].at[pl.ds(first, n)], m_s.at[pl.ds(at, n)], m_sem.at[i]
            )
            for i, (k, first, n, at) in enumerate(m_places)
        ]
        copies_c = [
            pltpu.make_async_copy(
                c_in.at[pl.ds(pl.multiple_of(table[i], each), each)],
                c_s.at[pl.ds(i * each, each)],
                c_sem.at[i],
            )
            for i in range(nc)
        ]
        c_places = [(0, 0, each, i * each) for i in range(nc)]
        g_copy = pltpu.make_async_copy(gate_in.at[pl.ds(row, rows)], gate_ref, w_sem.at[2])
        w_gu = pltpu.make_async_copy(gu_in, gu_w, w_sem.at[0])
        w_dn = pltpu.make_async_copy(dn_in, dn_w, w_sem.at[1])
        def of_block(copies, places, b):
            return [c for c, p in zip(copies, places) if b * step <= p[3] < (b + 1) * step]

        for c in of_block(copies_m, m_places, 0):
            c.start()
        w_gu.start()
        g_copy.start()

        def sends(b):
            here = pl.ds(b * step, step)
            return [
                pltpu.make_async_copy(dmx_s.at[here], dmx_out.at[here], o_sem.at[2 * b]),
                pltpu.make_async_copy(mix_s.at[here], mix_out.at[here], o_sem.at[2 * b + 1]),
            ]

        n = 2 * steps
        whole = [
            pltpu.make_async_copy(m_s, m_out, o_sem.at[n]),
            pltpu.make_async_copy(c_s, c_out, o_sem.at[n + 1]),
            pltpu.make_async_copy(hid_s, hid_out, o_sem.at[n + 2]),
            pltpu.make_async_copy(dgu_s, dgu_out, o_sem.at[n + 3]),
        ]

        def block(b, carry):
            r = pl.ds(pl.multiple_of(b * step, step), step)
            for k in range(steps):

                @pl.when(b == k)
                def _():
                    for c in of_block(copies_m, m_places, k):
                        c.wait()
                    if k == 0:
                        w_gu.wait()
                        g_copy.wait()
                        w_dn.start()
                        for c in of_block(copies_c, c_places, 0):
                            c.start()
                    if k + 1 < steps:
                        for c in of_block(copies_m, m_places, k + 1):
                            c.start()

            g_s[...] = times(m_s[r, :], gu_w[...])
            for k in range(steps):

                @pl.when(b == k)
                def _():
                    for c in of_block(copies_c, c_places, k):
                        c.wait()
                    if k == 0:
                        w_dn.wait()
                    if k + 1 < steps:
                        for c in of_block(copies_c, c_places, k + 1):
                            c.start()
                    else:
                        whole[0].start()
                        whole[1].start()

            q_s[...] = times_transposed(c_s[r, :], dn_w[...])
            for s in range(step // small):
                here = slice(s * small, (s + 1) * small)
                out = pl.ds(pl.multiple_of(b * step + s * small, small), small)
                scale = gate_ref[out, :]
                g = g_s[here, :hidden]
                u = g_s[here, hidden:]
                q = q_s[here, :]
                sig = jax.nn.sigmoid(g)
                act = g * sig
                hid = act * u
                dots_ref[out, :] = jnp.sum(hid * q, axis=1, keepdims=True)
                hid_s[out, :] = (hid * scale).astype(BF16)
                dh = q * scale
                dgu_s[out, :hidden] = (dh * u * (sig + act * (1.0 - sig))).astype(BF16)
                dgu_s[out, hidden:] = (dh * act).astype(BF16)
            dmx_s[r, :] = times_transposed(dgu_s[r, :], gu_w[...]).astype(BF16)
            mix_s[r, :] = times(hid_s[r, :], dn_w[...]).astype(BF16)
            for k in range(steps):

                @pl.when(b == k)
                def _():
                    for c in sends(k):
                        c.start()

            return carry

        lax.fori_loop(0, steps, block, 0)
        whole[2].start()
        whole[3].start()
        for c in whole + [c for k in range(steps) for c in sends(k)]:
            c.wait()

    anywhere = pl.BlockSpec(memory_space=pl.ANY)
    vmem = pl.BlockSpec(memory_space=pltpu.VMEM)
    sds = jax.ShapeDtypeStruct
    return pl.pallas_call(
        kernel,
        out_shape=[
            sds((rows, width), BF16),
            sds((rows, width), BF16),
            sds((rows, 1), F32),
            sds((rows, width), BF16),
            sds((rows, width), BF16),
            sds((rows, hidden), BF16),
            sds((rows, 2 * hidden), BF16),
        ],
        in_specs=[anywhere] * (nm + 1)
        + [pl.BlockSpec(memory_space=pltpu.SMEM)]
        + [anywhere] * 3,
        out_specs=[anywhere] * 2 + [vmem] + [anywhere] * 4,
        scratch_shapes=[
            pltpu.VMEM((rows, width), BF16),
            pltpu.VMEM((rows, width), BF16),
            pltpu.VMEM((width, 2 * hidden), BF16),
            pltpu.VMEM((hidden, width), BF16),
            pltpu.VMEM((rows, hidden), BF16),
            pltpu.VMEM((rows, width), BF16),
            pltpu.VMEM((rows, width), BF16),
            pltpu.VMEM((rows, 2 * hidden), BF16),
            pltpu.VMEM((step, 2 * hidden), F32),
            pltpu.VMEM((step, hidden), F32),
            pltpu.VMEM((rows, 1), F32),
            pltpu.SemaphoreType.DMA((len(m_places),)),
            pltpu.SemaphoreType.DMA((nc,)),
            pltpu.SemaphoreType.DMA((3,)),
            pltpu.SemaphoreType.DMA((2 * steps + 4,)),
        ],
        compiler_params=pltpu.CompilerParams(vmem_limit_bytes=60 << 20),
        cost_estimate=pl.CostEstimate(
            flops=2 * rows * width * hidden * 6, bytes_accessed=24 << 20, transcendentals=0
        ),
    )(*m_arrays, c_all, c_rows, gates, gu, down)


def attention_specs(length, heads, head_width, step):
    rows = pl.BlockSpec((step, head_width), lambda h, i: (i, h))
    whole = pl.BlockSpec((length, head_width), lambda h, i: (0, h))
    marks = pl.BlockSpec((step, 2), lambda h, i: (i, 0))
    marks_t = pl.BlockSpec((2, length), lambda h, i: (0, 0))
    sums = pl.BlockSpec((1, step, 1), lambda h, i: (h, i, 0))
    return rows, whole, marks, marks_t, sums


def pair_scores(q, k, marks, marks_t, scale):
    scores = times_transposed(q, k) * scale
    allowed = (marks_t[0:1, :] <= marks[:, 0:1]) & (marks_t[1:2, :] == marks[:, 1:2])
    return scores, allowed


def turn(values, cosine, sine):
    return values * cosine + pltpu.roll(values, values.shape[1] // 2, 1) * sine


def turn_back(values, cosine, sine):
    return values * cosine + pltpu.roll(values * sine, values.shape[1] // 2, 1)


def attention(qkv, inverse, gains, tables, marks, heads, scale):
    length, width = qkv.shape[0], gains.shape[1]
    head_width, step = width // heads, 256

    def kernel(q_ref, k_ref, v_ref, qi_ref, ki_ref, qg_ref, cq_ref, sq_ref, ck_ref, sk_ref,
               marks_ref, marks_t_ref, o_ref, sum_ref, q_out, k_out):
        @pl.when(pl.program_id(1) == 0)
        def _():
            scaled = k_ref[...] * ki_ref[:, 1:2] * qg_ref[1:2, :]
            k_out[...] = turn(scaled, ck_ref[...], sk_ref[...]).astype(BF16)

        scaled = q_ref[...] * qi_ref[:, 0:1] * qg_ref[0:1, :]
        q = turn(scaled, cq_ref[...], sq_ref[...]).astype(BF16)
        q_out[...] = q
        scores, allowed = pair_scores(q, k_out[...], marks_ref[...], marks_t_ref[...], scale)
        scores = jnp.where(allowed, scores, -1e30)
        top = jnp.max(scores, axis=1, keepdims=True)
        terms = jnp.where(allowed, jnp.exp(scores - top), 0.0)
        total = jnp.sum(terms, axis=1, keepdims=True)
        probs = terms * (1.0 / total)
        o_ref[...] = times(probs.astype(BF16), v_ref[...].astype(BF16)).astype(BF16)
        sum_ref[0] = top + jnp.log(total)

    rows, whole, marks_s, marks_ts, sums = attention_specs(length, heads, head_width, step)
    turned = pl.BlockSpec((step, head_width), lambda h, i: (i, 0))
    turned_all = pl.BlockSpec((length, head_width), lambda h, i: (0, 0))
    return pl.pallas_call(
        kernel,
        grid=(heads, length // step),
        out_shape=[
            jax.ShapeDtypeStruct((length, width), BF16),
            jax.ShapeDtypeStruct((heads, length, 1), F32),
            jax.ShapeDtypeStruct((length, width), BF16),
            jax.ShapeDtypeStruct((length, width), BF16),
        ],
        in_specs=[
            rows,
            pl.BlockSpec((length, head_width), lambda h, i: (0, heads + h)),
            pl.BlockSpec((length, head_width), lambda h, i: (0, 2 * heads + h)),
            marks_s,
            pl.BlockSpec((length, 2), lambda h, i: (0, 0)),
            pl.BlockSpec((2, head_width), lambda h, i: (0, h)),
            turned,
            turned,
            turned_all,
            turned_all,
            marks_s,
            marks_ts,
        ],
        out_specs=[rows, sums, rows, whole],
        compiler_params=pltpu.CompilerParams(vmem_limit_bytes=48 << 20),
        cost_estimate=pl.CostEstimate(
            flops=4 * length * length * width, bytes_accessed=4 << 20, transcendentals=0
        ),
    )(qkv, qkv, qkv, inverse, inverse, gains, *tables, *tables, marks, marks.T)


def attention_back(query, key, qkv, grad, log_sums, tables, marks, heads, scale):
    length, width = query.shape
    head_width, step = width // heads, 256

    def kernel(q_ref, k_ref, v_ref, do_ref, sum_ref, cq_ref, sq_ref, ck_ref, sk_ref, marks_ref,
               marks_t_ref, dq_ref, dk_ref, dv_ref):
        q, k, do = q_ref[...], k_ref[...], do_ref[...]
        scores, allowed = pair_scores(q, k, marks_ref[...], marks_t_ref[...], scale)
        probs = jnp.where(allowed, jnp.exp(scores - sum_ref[0]), 0.0)
        grad_p = times_transposed(do, v_ref[...].astype(BF16))
        delta = jnp.sum(probs * grad_p, axis=1, keepdims=True)
        grad_s = (probs * (grad_p - delta)).astype(BF16)
        dq_ref[...] = turn_back(times(grad_s, k) * scale, cq_ref[...], sq_ref[...])
        dk = rows_by_rows(grad_s, q) * scale
        dv = rows_by_rows(probs.astype(BF16), do)
        first = pl.program_id(1) == 0

        @pl.when(first)
        def _():
            dk_ref[...] = dk
            dv_ref[...] = dv

        @pl.when(jnp.logical_not(first))
        def _():
            dk_ref[...] += dk
            dv_ref[...] += dv

        @pl.when(pl.program_id(1) == length // step - 1)
        def _():
            dk_ref[...] = turn_back(dk_ref[...], ck_ref[...], sk_ref[...])

    rows, whole, marks_s, marks_ts, sums = attention_specs(length, heads, head_width, step)
    return pl.pallas_call(
        kernel,
        grid=(heads, length // step),
        out_shape=[jax.ShapeDtypeStruct((length, width), F32)] * 3,
        in_specs=[
            rows,
            whole,
            pl.BlockSpec((length, head_width), lambda h, i: (0, 2 * heads + h)),
            rows,
            sums,
            pl.BlockSpec((step, head_width), lambda h, i: (i, 0)),
            pl.BlockSpec((step, head_width), lambda h, i: (i, 0)),
            pl.BlockSpec((length, head_width), lambda h, i: (0, 0)),
            pl.BlockSpec((length, head_width), lambda h, i: (0, 0)),
            marks_s,
            marks_ts,
        ],
        out_specs=[rows, whole, whole],
        compiler_params=pltpu.CompilerParams(vmem_limit_bytes=48 << 20),
        cost_estimate=pl.CostEstimate(
            flops=10 * length * length * width, bytes_accessed=8 << 20, transcendentals=0
        ),
    )(query, key, qkv, grad, log_sums, *tables, *tables, marks, marks.T)


def gate_up_weights(lefts, rights, before=None, rest=None):
    rows, width = lefts[0].shape
    cols = rights[0].shape[1]
    n, tile = len(lefts), 512
    steps = width // tile // 2
    skip = 0 if rest is None else steps

    def kernel(*refs):
        total = rows_by_rows(refs[0][...], refs[n][...])
        for i in range(1, n):
            total = total + rows_by_rows(refs[i][...], refs[n + i][...])
        out = refs[-1]
        for k in range(2):
            part = total[:, k * (cols // 2) : (k + 1) * (cols // 2)]
            out[:, k, :] = part if before is None else part + refs[2 * n][:, k, :]

    block = pl.BlockSpec((tile, 2, cols // 2), lambda i: (i + skip, 0, 0))
    extra = [] if before is None else [before]
    old = [] if rest is None else [rest]
    return pl.pallas_call(
        kernel,
        grid=(steps,),
        out_shape=jax.ShapeDtypeStruct((width, 2, cols // 2), F32),
        in_specs=[pl.BlockSpec((rows, tile), lambda i: (0, i + skip))] * n
        + [pl.BlockSpec((rows, cols), lambda i: (0, 0))] * n
        + [block] * len(extra)
        + [pl.BlockSpec(memory_space=pl.ANY)] * len(old),
        out_specs=block,
        input_output_aliases={2 * n + len(extra): 0} if old else {},
        compiler_params=pltpu.CompilerParams(vmem_limit_bytes=58 << 20),
        cost_estimate=pl.CostEstimate(
            flops=n * rows * width * cols, bytes_accessed=16 << 20, transcendentals=0
        ),
    )(*lefts, *rights, *extra, *old)


def down_weights(lefts, rights, before=None):
    rows, hidden = lefts[0].shape
    width = rights[0].shape[1]
    n, tile = len(lefts), 512

    def kernel(*refs):
        total = rows_by_rows(refs[0][...], refs[n][...])
        for i in range(1, n):
            total = total + rows_by_rows(refs[i][...], refs[n + i][...])
        refs[-1][...] = total if before is None else total + refs[2 * n][...]

    block = pl.BlockSpec((hidden, tile), lambda i: (0, i))
    extra = [] if before is None else [before]
    return pl.pallas_call(
        kernel,
        grid=(width // tile,),
        out_shape=jax.ShapeDtypeStruct((hidden, width), F32),
        in_specs=[pl.BlockSpec((rows, hidden), lambda i: (0, 0))] * n
        + [pl.BlockSpec((rows, tile), lambda i: (0, i))] * n
        + [block] * len(extra),
        out_specs=block,
        compiler_params=pltpu.CompilerParams(vmem_limit_bytes=58 << 20),
        cost_estimate=pl.CostEstimate(
            flops=2 * n * rows * width * hidden, bytes_accessed=24 << 20, transcendentals=0
        ),
    )(*lefts, *rights, *extra)


def after(x, *others):
    return lax.optimization_barrier((x, *others))[0]


def flip_slots(x, size, me):
    n = len(link_bits(size)) + 1
    for axis, b in enumerate([1] + link_bits(size)[::-1]):
        x = jnp.where((me & b) != 0, jnp.flip(x, axis), x)
    return x, n


def to_slots(x, size, me):
    n = len(link_bits(size)) + 1
    y = jnp.moveaxis(x.reshape((2,) * n + x.shape[1:]), n - 1, 0)
    return flip_slots(y, size, me)[0].reshape(x.shape)


def from_slots(x, size, me):
    n = len(link_bits(size)) + 1
    y = flip_slots(x.reshape((2,) * n + x.shape[1:]), size, me)[0]
    return jnp.moveaxis(y, 0, n - 1).reshape(x.shape)


def sum_to_owners(x, planes, size, plane, place):
    n, _, rows = x.shape
    for axis, count, me in (("seq", size, place), ("fsdp", planes, plane)):
        outer = planes if axis == "seq" else 1
        b = 1
        while b < count:
            y = x.reshape(n, outer, -1, 2, rows)
            high = (me & b) != 0
            mine = jnp.where(high, y[:, :, :, 1], y[:, :, :, 0])
            theirs = jnp.where(high, y[:, :, :, 0], y[:, :, :, 1])
            x = mine + lax.ppermute(theirs, axis, [(i, i ^ b) for i in range(count)])
            x = x.reshape(n, -1, rows)
            b *= 2
    return x[:, 0]


def per_device(
    tokens,
    segments,
    routes,
    out_grad,
    w_query,
    w_key,
    w_value,
    w_out,
    router,
    attn_gain,
    q_gain,
    k_gain,
    ffn_gain,
    expert_gate_up,
    expert_down,
):
    F, S = lax.axis_size("fsdp"), lax.axis_size("seq")
    N = F * S
    experts = N // SPLIT
    R, D = tokens.shape
    HW = D // HEADS
    HL = HEADS // S
    CW = HL * HW
    RW = w_query.shape[0]
    L = S * R
    scale = HW ** (-0.5)
    me_f, me_s = lax.axis_index("fsdp"), lax.axis_index("seq")
    me = me_f * S + me_s
    order = mask_order(S)
    slots = jnp.stack([me_s ^ m for m in order + [m | 1 for m in order]])

    def shift_in(x, j):
        return lax.ppermute(x, "fsdp", [((i + j) % F, i) for i in range(F)])

    def shift_back(x, j):
        return lax.ppermute(x, "fsdp", [(i, (i + j) % F) for i in range(F)])

    def in_order(pieces):
        return [a for m in order for a in pieces[m]]

    def sequence_rows(x):
        mine = gather_pieces(x, S)
        return jnp.concatenate(in_order(mine) + in_order(other_core(mine, S)))

    w_low = jnp.stack([w.astype(BF16) for w in (w_query, w_key, w_value)], axis=1)
    w_send = w_low.reshape(RW, 3, S, CW).transpose(2, 0, 1, 3).reshape(S, RW, 3 * CW)
    w_mine = lax.all_to_all(w_send, "seq", split_axis=0, concat_axis=0, tiled=True)
    w_mine = w_mine.reshape(S * RW, 3 * CW)
    wo_all = lax.all_gather(w_out.astype(BF16), BOTH, axis=0, tiled=True)
    c_all = lax.all_gather(after(out_grad, w_mine), BOTH, axis=0, tiled=True)
    expert = me // SPLIT
    unit = R // 2
    z_order = sorted(range(1, F), key=lambda j: (-min(j, F - j), j))
    hidden_width = expert_down.shape[1]
    gu_low = after(expert_gate_up, w_mine)[0].astype(BF16).reshape(D, 2 * hidden_width)
    down_low = after(expert_down, w_mine)[0].astype(BF16)

    up = down = w_mine
    ups, downs = [], []
    x_first = gather_first(after(tokens, w_mine), S)
    x_both = []
    for k in range(F - 1):
        up = lax.ppermute(up, "fsdp", [(i, i + 1) for i in range(F - 1)])
        down = lax.ppermute(down, "fsdp", [(i + 1, i) for i in range(F - 1)])
        ups.append(up)
        downs.append(down)
        if k == 0:
            keys = list(x_first)
            up, down, *got = lax.optimization_barrier(
                (up, down, *[x_first[m][0] for m in keys])
            )
            x_first = {m: [a] for m, a in zip(keys, got)}
            x_mine = gather_rest(x_first, S)
            x_other = other_core(x_first, S)
        elif k == 1:
            near = flat(x_other)
            far_keys = [m for m in x_mine if m not in x_first]
            far = [a for m in far_keys for a in x_mine[m]]
            up, down, *got = lax.optimization_barrier((up, down, *far, *near))
            far, near = got[: len(far)], got[len(far) :]
            x_other = {m: [a] for m, a in zip(keys, near)}
            for i, m in enumerate(far_keys):
                x_mine[m] = far[2 * i : 2 * i + 2]
                x_other[m] = [exchange(a, 1, S) for a in x_mine[m]]
        else:
            up, down = lax.optimization_barrier((up, down))
    x_seq = jnp.concatenate(in_order(x_mine) + in_order(x_other)).astype(F32)
    gains = jnp.stack([attn_gain, q_gain, k_gain, ffn_gain])
    small = [gains.astype(BF16), router.T.astype(BF16), segments.astype(BF16)]
    sizes = [4 * RW, experts * RW, R]
    pad = jnp.zeros((-sum(sizes) % 128,), BF16)
    small = jnp.concatenate([a.reshape(-1) for a in small] + [pad]).reshape(1, -1, 128)
    small = after(small, ups[min(1, F - 2)])
    small = jnp.broadcast_to(small, (N,) + small.shape[1:])
    small = lax.all_to_all(small, BOTH, split_axis=0, concat_axis=0, tiled=True).reshape(N, -1)
    parts, at = [], 0
    for n in sizes:
        parts.append(small[:, at : at + n])
        at += n
    gains_all = parts[0].reshape(N, 4, RW).transpose(1, 0, 2).reshape(4, D).astype(F32)
    ga, gq, gk, gf = [gains_all[i] for i in range(4)]
    router_t = parts[1].reshape(N, experts, RW).transpose(1, 0, 2).reshape(experts, D)
    segment_all = lax.dynamic_slice(parts[2].astype(F32), (me_f * S, 0), (S, R))

    x_inverse = inverse_rms(x_seq)
    a_seq = after((x_seq * x_inverse * ga).astype(BF16), gu_low, down_low)
    cols = 3 * CW
    w_cols = jnp.concatenate(ups[::-1] + [w_mine] + downs)
    w_cols = lax.dynamic_slice(w_cols, ((F - 1 - me_f) * S * RW, 0), (D, cols))
    qkv = times(a_seq, w_cols)
    q_proj, k_proj = qkv[:, :CW], qkv[:, CW : 2 * CW]

    def seq_sum(stats):
        stats = stats.reshape(-1, 2, S // 2, R)
        total = stats + exchange(stats, 1, S)[:, ::-1]
        for b in link_bits(S):
            other = exchange(total, b, S)
            total = total + jnp.stack([other[:, :, order.index(m ^ b)] for m in order], axis=2)
        return total.reshape(-1, L)

    squares = seq_sum(jnp.stack([jnp.sum(q_proj * q_proj, 1), jnp.sum(k_proj * k_proj, 1)]))
    inverse = lax.rsqrt(squares / D + EPSILON)
    q_inv, k_inv = inverse[0][:, None], inverse[1][:, None]
    gq_mine = lax.dynamic_slice(gq, (me_s * CW,), (CW,))
    gk_mine = lax.dynamic_slice(gk, (me_s * CW,), (CW,))
    positions = (slots[:, None] * R + jnp.arange(R, dtype=jnp.int32)[None]).reshape(L)
    segment_seq = to_slots(segment_all, S, me_s).reshape(L)
    cosine, sine = [t[:, 0] for t in rope_tables(positions, HW)]
    tables = (
        jnp.concatenate([cosine, cosine], axis=1),
        jnp.concatenate([-sine, sine], axis=1),
    )
    marks = jnp.stack([positions.astype(F32), segment_seq], axis=1)
    gains_mine = jnp.stack([gq_mine, gk_mine])
    attended, log_sums, query, key = attention(
        qkv, inverse.T, gains_mine, tables, marks, HL, scale
    )
    o_send = attended.reshape(S, R, CW)
    o_send = from_slots(o_send, S, me_s)
    o_mine = lax.all_to_all(o_send, "seq", split_axis=0, concat_axis=0, tiled=True)
    o_mine = o_mine.transpose(1, 0, 2).reshape(R, D)
    middle = tokens.astype(F32) + times(o_mine, wo_all)
    mid_inv = inverse_rms(middle)
    mixed = (middle * mid_inv * gf).astype(BF16)
    expert_probs = jax.nn.softmax(times_transposed(mixed, router_t), axis=-1)

    chosen = routes[:, :, None] == jnp.arange(experts, dtype=jnp.int32)
    named = jnp.any(chosen, axis=1).astype(F32)
    gates = jnp.repeat((expert_probs * named).T, SPLIT, axis=0)
    gates = lax.all_to_all(gates, BOTH, split_axis=0, concat_axis=0, tiled=True).reshape(F, S, R)
    b = 1
    while b < F:
        gates = jnp.where((me_f & b) != 0, jnp.roll(gates, -b, axis=0), gates)
        b *= 2
    m_far, last = {0: mixed}, mixed
    for j in z_order:
        last = shift_in(after(mixed, last), j)
        m_far[j] = last
    chunks = [0] + z_order
    first = {j: gather_first(m_far[j], S) for j in chunks}
    mine = {j: gather_one_way(first[j], S, i % 2) for i, j in enumerate(chunks)}
    mine[0] = gather_rest(first[0], S)
    both = {j: [mine[j], other_core(mine[j], S)] for j in chunks}
    last_chunk = chunks[-1]
    top_level = len(link_bits(S))
    calls = [(j, side) for j in chunks for side in ((1, 0) if j == last_chunk else (0, 1))]
    tick = {call: t for t, call in enumerate(calls)}
    before = {t: [] for t in range(len(calls) + 4)}
    for i, j in enumerate(chunks):
        early = 1 if j == last_chunk else 0
        t = 2 * i
        before[max(t - 2 - early, 0)].append(m_far[j])
        before[max(t - 1 - early, 0)] += flat(first[j])
        before[max(t - early, 0)] += flat(mine[j])
        before[max(t + 1 - early, 0)] += flat(both[j][1])
    c_rows = (me_f + jnp.arange(F, dtype=jnp.int32)) % F * S
    c_rows = (c_rows[:, None] + slots[None]).reshape(F, 2, S // 2) * R
    finished, kept, dots = {}, [], {}
    gate_up_grad, down_grad = None, None

    def flush(kept, gate_up_grad, down_grad):
        ms, cs, hids, dgus = [list(a) for a in zip(*kept)]
        down_grad = down_weights(hids, cs, down_grad)
        first = gate_up_weights(ms, dgus, gate_up_grad)
        return gate_up_weights(ms, dgus, gate_up_grad, first), down_grad

    def last_flush(at, level):
        ms, cs, hids, dgus = [list(a) for a in zip(*kept)]
        if level == 1:
            hids[0] = after(hids[0], *before[at])
            done["down"] = down_weights(hids, cs, down_grad)
            return [done["down"]]
        ms[0] = after(ms[0], *before[at + 1], *before[at + 2], *before[at + 3])
        done["gate_up"] = gate_up_weights(ms, dgus, gate_up_grad)
        return [done["gate_up"]]

    done = {}
    mix_sides, dmx_sides, mix_got, mix_done = {}, {}, {}, {}
    gate_rows = jnp.stack([to_slots(gates[j], S, me_s) for j in range(F)]).reshape(F * L, 1)
    for t, (j, side) in enumerate(calls):
        m_parts = [(a, 0, a.shape[0]) for m in order for a in both[j][side][m]]
        m_parts[0] = (after(m_parts[0][0], *before[t]), *m_parts[0][1:])
        row = j * L + side * (L // 2)
        mix, dmx, dot, *saved = expert_rows(
            m_parts, c_all, c_rows[j, side], gate_rows, row, gu_low, down_low
        )
        mix_sides[j, side], dmx_sides[j, side] = mix, dmx
        dots[j, side] = dot.reshape(-1)
        kept.append(saved)
        if F > 4 and len(kept) == 8 and t + 2 < len(calls):
            gate_up_grad, down_grad = flush(kept, gate_up_grad, down_grad)
            before[t + 2] += [gate_up_grad, down_grad]
            kept = []
        if side:
            mix_got[j] = exchange(mix, 1, S)
            before[t + 3].append(mix_got[j])
        if (j, 1 - side) in dmx_sides:
            given = tick[j, 1]

            def hold(level, sums):
                before[min(given + 2 + top_level - level, len(calls) + 3)].extend(sums)
                return sums

            ties = None
            if j == last_chunk:
                ties = {n: lambda n=n: last_flush(len(calls), n) for n in (0, 1)}

            way = chunks.index(j) % 2
            both_sums = [(dmx_sides[j, 0], exchange(dmx_sides[j, 1], 1, S), 1, 0, way)]
            both_sums.append((mix_sides.pop((j, 0)), mix_got.pop(j), 1, 0, 1 - way))
            total, mix = scatter_sum(both_sums, S, R, [BF16 if j else F32, BF16], hold, ties)
            mix_done[j] = shift_back(mix, j) if j else mix
            before[min(given + 5, len(calls) + 3)].append(mix_done[j])
            finished[j] = shift_back(total, j) if j else total
            last_sum = total
    dots = {j: jnp.concatenate([dots[j, 0], dots[j, 1]]).reshape(S, R) for j in chunks}
    dots = [dots[j] for j in range(F)]
    finished = [finished[j] for j in range(F)]
    dmx_total = finished[0]
    for t in finished[1:]:
        dmx_total = dmx_total + t.astype(F32)
    ms, _, _, dgus = [list(a) for a in zip(*kept)]
    ms[0] = after(ms[0], last_sum)
    gate_up_grad = gate_up_weights(ms, dgus, gate_up_grad, done["gate_up"])
    down_grad = done["down"]
    dmx_total = after(dmx_total, gate_up_grad)
    expert_gate_up_grad, expert_down_grad = gate_up_grad[None], down_grad[None]
    dots = jnp.stack([from_slots(d, S, me_s) for d in dots])
    b = 1
    while b < F:
        dots = jnp.where((me_f & b) != 0, jnp.roll(dots, b, axis=0), dots)
        b *= 2
    dots = dots.reshape(N, R)
    dots = lax.all_to_all(dots, BOTH, split_axis=0, concat_axis=0, tiled=True)
    dots = after(dots, gate_up_grad)
    grad_probs = jnp.sum(dots.reshape(experts, SPLIT, R), axis=1).T * named
    grad_logits = expert_probs * (
        grad_probs - jnp.sum(expert_probs * grad_probs, axis=-1, keepdims=True)
    )
    grad_logits = grad_logits.astype(BF16)
    router_part = rows_by_rows(grad_logits, mixed)
    grad_mixed = dmx_total + times(grad_logits, router_t)

    grad_output = out_grad.astype(F32)
    scaled = grad_mixed * gf
    grad_middle = (
        grad_output
        + mid_inv * scaled
        - middle * mid_inv**3 * jnp.mean(scaled * middle, axis=-1, keepdims=True)
    )
    ffn_part = jnp.sum(grad_mixed * middle * mid_inv, axis=0)
    early = jnp.concatenate([router_part, ffn_part[None]]).reshape(experts + 1, N, RW)
    early = sum_to_owners(early, F, S, me_f, me_s)
    router_grad = early[:experts].T
    ffn_grad = early[experts]

    proj_low = grad_middle.astype(BF16)
    grad_proj = sequence_rows(proj_low)
    out_part = rows_by_rows(attended, grad_proj).astype(BF16)
    out_sum = lax.psum_scatter(out_part, "fsdp", scatter_dimension=0, tiled=True)
    pairs = [(f * S + s, F * s + f) for f in range(F) for s in range(S)]
    out_grad_total = lax.ppermute(out_sum, BOTH, pairs).astype(F32)
    output = middle
    for j in chunks:
        output = output + mix_done[j].astype(F32)
    output = output.astype(BF16)

    wo_rows = lax.dynamic_slice(wo_all, (me_s * CW, 0), (CW, D))
    grad_heads = times_transposed(
        after(grad_proj, out_part, early, *mix_done.values()), wo_rows
    ).astype(BF16)
    dq, dk, dv = attention_back(
        query, key, qkv, grad_heads, log_sums, tables, marks, HL, scale
    )
    q_part = jnp.sum(dq * q_proj * q_inv, axis=0)
    k_part = jnp.sum(dk * k_proj * k_inv, axis=0)
    dq = dq * gq_mine
    dk = dk * gk_mine
    means = jnp.stack([jnp.sum(dq * q_proj, 1), jnp.sum(dk * k_proj, 1)])
    means = seq_sum(means) / D
    dqp = q_inv * dq - q_proj * q_inv**3 * means[0][:, None]
    dkp = k_inv * dk - k_proj * k_inv**3 * means[1][:, None]
    dv_low = dv.astype(BF16)
    dqk = jnp.concatenate([dqp.astype(BF16), dkp.astype(BF16)], axis=1)
    v_part = rows_by_rows(a_seq, dv_low).astype(BF16)
    v_sum = lax.psum_scatter(v_part, "fsdp", scatter_dimension=0, tiled=True)
    qk_part = rows_by_rows(a_seq, after(dqk, v_part)).astype(BF16).reshape(N, RW, 2 * CW)
    qk_got = lax.all_to_all(qk_part, BOTH, split_axis=0, concat_axis=0, tiled=True)
    qk_parts = qk_got.reshape(F, S, RW, 2 * CW)
    qk_all = qk_parts[0].astype(F32)
    for f in range(1, F):
        qk_all = qk_all + qk_parts[f].astype(F32)
    qk_sum = [
        qk_all[:, :, i * CW : (i + 1) * CW].transpose(1, 0, 2).reshape(RW, D) for i in range(2)
    ]
    v_got = lax.all_to_all(
        after(v_sum, qk_got).reshape(S, RW, CW), "seq", split_axis=0, concat_axis=0, tiled=True
    )
    w_sum = [qk_sum[0], qk_sum[1], v_got.transpose(1, 0, 2).reshape(RW, D).astype(F32)]
    dqkv = jnp.concatenate([after(dqk, qk_part), dv_low], axis=1)
    x_scaled = x_seq * x_inverse
    da_keep = times_transposed(dqkv[: L // 2], w_cols)
    da_give = times_transposed(dqkv[L // 2 :], w_cols)
    attn_part = jnp.sum(da_keep * x_scaled[: L // 2], axis=0) + jnp.sum(
        da_give * x_scaled[L // 2 :], axis=0
    )
    da_keep = da_keep.astype(BF16)
    da_got = exchange(da_give.astype(BF16), 1, S)
    da_mine = jnp.concatenate(
        scatter_sum([(da_keep, da_got, 2, h, h) for h in range(2)], S, unit, [F32] * 2)
    )
    late = jnp.stack(
        [
            attn_part,
            lax.dynamic_update_slice(jnp.zeros((D,), F32), q_part, (me_s * CW,)),
            lax.dynamic_update_slice(jnp.zeros((D,), F32), k_part, (me_s * CW,)),
        ]
    )
    late = late.reshape(3, N, RW).transpose(1, 0, 2)
    late = lax.all_to_all(late, BOTH, split_axis=0, concat_axis=0, tiled=True)
    late = jnp.sum(late, axis=0)

    x = tokens.astype(F32)
    x_inv = inverse_rms(x)
    scaled = da_mine * ga
    grad_in = (
        grad_middle
        + x_inv * scaled
        - x * x_inv**3 * jnp.mean(scaled * x, axis=-1, keepdims=True)
    )
    return (
        output,
        grad_in.astype(BF16),
        w_sum[0],
        w_sum[1],
        w_sum[2],
        out_grad_total,
        router_grad,
        late[0],
        late[1],
        late[2],
        ffn_grad,
        expert_gate_up_grad,
        expert_down_grad,
    )


def solution(mesh):
    one, two = P(BOTH), P(BOTH, None)
    three, four = P(BOTH, None, None), P(BOTH, None, None, None)
    return jax.shard_map(
        per_device,
        mesh=mesh,
        in_specs=(two, one, two, two, two, two, two, two, two, one, one, one, one, four, three),
        out_specs=(two, two, two, two, two, two, two, one, one, one, one, four, three),
        check_vma=False,
    )
```
